256 devices in a mesh: section: 2 (over x_lo), row: 4 (over x_hi, core), col: 32 (over z, y).
Axes of the slice: x: 4 (x_hi: 2, x_lo: 2; x = x_hi * 2 + x_lo), y: 4, z: 8, core: 2. Of those that a mesh axis runs over, the one named last changes fastest.
Arguments:
- tokens: bfloat16 [1024, 4096], P('col', 'row'), may hold values from -6 to 6
- w_up: bfloat16 [2, 4096, 16384], P('section', 'row', 'col'), may hold values from -0.09375 to 0.09375
- w_down: bfloat16 [2, 16384, 4096], P('section', 'col', 'row'), may hold values from -0.046875 to 0.046875
- cotangent: bfloat16 [1024, 4096], P('row'), may hold values from -0.23925781 to 0.23925781
Outputs:
- grad_up: float32 [2, 4096, 16384], P('section', 'row', 'col')
- grad_down: float32 [2, 16384, 4096], P('section', 'col', 'row')
The draws below stay inside these ranges and needn't reach their ends.
All inputs are finite; a program needn't handle non-finite values.
Results may differ from the reference program's by a relative error of at most 0.025.
Values may be sent and summed in bfloat16 or wider, within the bound.
No kernel may reach another device: no remote copies, remote signals or barrier semaphores. Data moves between devices by JAX's collectives and lax.ppermute only.
A program may use at most 128 MiB of HBM per device.

```python
import jax
import jax.numpy as jnp
from jax import lax

D = 4096
FF = 16384
TOKENS = 1024
N_ROW = 4
N_COL = 32


def level_of(rng, dims, shards, smallest, high):
    def one(axis_at, shards_of):
        steps = jax.random.uniform(jax.random.fold_in(jax.random.fold_in(rng, 6), axis_at), (shards_of,), jnp.float32, smallest / len(shards), high / len(shards))
        return jnp.repeat(jnp.exp(steps), dims[axis_at] // shards_of).reshape((-1,) + (1,) * (len(dims) - axis_at - 1))

    gain = one(*shards[0])
    for cut in shards[1:]:
        gain = gain * one(*cut)
    return gain


def noise(stream_key, extent, spread, most, split=(), held_as=jnp.bfloat16):
    gain = level_of(stream_key, extent, split, -0.22, 0.18) if split else 1.0
    array = jax.random.normal(stream_key, extent, jnp.float32) * spread * gain
    return jnp.minimum(jnp.maximum(array, -most), most).astype(held_as)


def setup_inputs(seed: int = 0) -> dict:
    key_list = jax.random.split(jax.random.key(seed), 5)
    tokens = noise(key_list[0], (TOKENS, D), 1.0, 6.0, ((0, 32), (1, 4)))
    w_up = noise(key_list[1], (2, D, FF), D ** -0.5, 0.09375, ((0, 2), (1, 4), (2, 32)))
    w_down = noise(key_list[2], (2, FF, D), FF ** -0.5, 0.046875, ((0, 2), (1, 32), (2, 4)))
    cotangent = noise(key_list[3], (TOKENS, D), 0.04, 0.23925781, ((0, 4),))
    return dict(tokens=tokens, w_up=w_up, w_down=w_down, cotangent=cotangent)


def gelu(values):
    return jax.nn.gelu(values, approximate=True)

def gelu_grad(values, upstream):
    return jax.vjp(gelu, values)[1](upstream)[0]

def block_products(left, right, blocks):
    width = left.shape[1] // blocks

    def step(total, index):
        start = (index * width).astype(jnp.int32)
        left_part = lax.dynamic_slice_in_dim(left, start, width, 1)
        right_part = lax.dynamic_slice_in_dim(right, start, width, 0)
        product = jnp.dot(left_part, right_part, preferred_element_type=jnp.float32)
        return (total + product.astype(jnp.bfloat16).astype(jnp.float32), None)
    total = jnp.zeros((left.shape[0], right.shape[1]), jnp.float32)
    total, unused = lax.scan(step, total, jnp.arange(blocks, dtype=jnp.int32))
    return total

def token_products(left, right, blocks):
    height = left.shape[0] // blocks

    def step(total, index):
        start = (index * height).astype(jnp.int32)
        left_part = lax.dynamic_slice_in_dim(left, start, height, 0)
        right_part = lax.dynamic_slice_in_dim(right, start, height, 0)
        product = lax.dot_general(left_part, right_part, (((0,), (0,)), ((), ())), preferred_element_type=jnp.float32)
        return (total + product.astype(jnp.bfloat16).astype(jnp.float32), None)
    total = jnp.zeros((left.shape[1], right.shape[1]), jnp.float32)
    total, unused = lax.scan(step, total, jnp.arange(blocks, dtype=jnp.int32))
    return total

def reference(tokens, w_up, w_down, cotangent):
    pre_a = jnp.dot(tokens, w_up[0], preferred_element_type=jnp.float32)
    hidden_a = gelu(pre_a).astype(jnp.bfloat16)
    out_sum = block_products(hidden_a, w_down[0], N_COL)
    boundary = (tokens.astype(jnp.float32) + out_sum).astype(jnp.bfloat16)
    pre_b = jnp.dot(boundary, w_up[1], preferred_element_type=jnp.float32)
    hidden_b = gelu(pre_b).astype(jnp.bfloat16)
    grad_hidden_b = jnp.dot(cotangent, w_down[1].T, preferred_element_type=jnp.float32)
    grad_pre_b = gelu_grad(pre_b, grad_hidden_b).astype(jnp.bfloat16)
    down_b = token_products(hidden_b, cotangent, N_ROW)
    up_b = token_products(boundary, grad_pre_b, N_ROW)
    back_sum = block_products(grad_pre_b, w_up[1].T, N_COL)
    grad_boundary = (cotangent.astype(jnp.float32) + back_sum).astype(jnp.bfloat16)
    grad_hidden_a = jnp.dot(grad_boundary, w_down[0].T, preferred_element_type=jnp.float32)
    grad_pre_a = gelu_grad(pre_a, grad_hidden_a).astype(jnp.bfloat16)
    down_a = lax.dot_general(hidden_a, grad_boundary, (((0,), (0,)), ((), ())), preferred_element_type=jnp.float32)
    up_a = lax.dot_general(tokens, grad_pre_a, (((0,), (0,)), ((), ())), preferred_element_type=jnp.float32)
    return (jnp.stack([up_a, up_b]), jnp.stack([down_a, down_b]))
```

```python
import jax
import jax.numpy as jnp
from jax import lax
from jax.sharding import PartitionSpec as P

NY = 4
NZ = 8
Z_NEAR = 1
Z_FAR = (2, 4, 6)
Y_STEPS = (1, 2, 3)


def gelu(values):
    return jax.nn.gelu(values, approximate=True)


def gelu_grad(values, upstream):
    return jax.vjp(gelu, values)[1](upstream)[0]


def swap_col(value, dz, dy):
    pairs = []
    for z in range(NZ):
        for y in range(NY):
            pairs.append((z * NY + y, (z ^ dz) * NY + (y ^ dy)))
    return lax.ppermute(value, "col", pairs)


def swap_section(value, dz):
    cols = NZ * NY
    pairs = []
    for s in range(2):
        for z in range(NZ):
            for y in range(NY):
                pairs.append((s * cols + z * NY + y, (1 - s) * cols + (z ^ dz) * NY + y))
    return lax.ppermute(value, ("section", "col"), pairs)


def swap_row(value, by):
    return lax.ppermute(value, "row", [(r, r ^ by) for r in range(4)])


def dot(left, right, dims):
    return lax.dot_general(left, right, (dims, ((), ())), preferred_element_type=jnp.float32)


def bf16(values):
    return values.astype(jnp.bfloat16)


def f32(values):
    return values.astype(jnp.float32)


def gather_z(shard):
    near = jnp.concatenate([shard] + [swap_col(shard, k, 0) for k in Z_FAR], 0)
    return jnp.concatenate([near, swap_col(near, Z_NEAR, 0)], 0)


def gather_y(block):
    return [block] + [swap_col(block, 0, k) for k in Y_STEPS]


def scatter_z_across(partial):
    half = partial.shape[0] // 2
    kept = bf16(f32(partial[:half]) + f32(swap_col(partial[half:], Z_NEAR, 0)))
    rows = half // 4
    total = f32(swap_section(kept[:rows], 0))
    for i, k in enumerate(Z_FAR):
        total = total + f32(swap_section(kept[(i + 1) * rows : (i + 2) * rows], k))
    return total


def reduce_row(partial, core):
    blocks, tokens, width = partial.shape
    halves = partial.reshape(blocks, 2, tokens // 2, width)
    mine = lax.dynamic_index_in_dim(halves, core, 1, False)
    other = lax.dynamic_index_in_dim(halves, 1 - core, 1, False)
    chip = f32(mine) + f32(swap_row(other, 1))
    return chip + f32(swap_row(bf16(chip), 2))


def join_cores(mine, core, axis):
    other = swap_row(mine, 1)
    first = jnp.where(core == 0, mine, other)
    second = jnp.where(core == 0, other, mine)
    return jnp.concatenate([first, second], axis)


def body(tokens, w_up, w_down, cotangent):
    first_section = lax.axis_index("section") == 0
    row = lax.axis_index("row")
    core = row % 2
    col = lax.axis_index("col")
    z = col // NY
    y = col % NY
    shard, width = tokens.shape
    up = w_up[0]
    down = w_down[0].T
    w_one = jnp.where(first_section, up, down)
    w_two = jnp.where(first_section, down, up)
    hidden_width = up.shape[1]

    rows = cotangent.shape[0] // (shard * NY)
    mine = lax.dynamic_index_in_dim(cotangent.reshape(rows, NY, shard, -1), y, 1, False)
    spread = lax.all_to_all(mine, "row", split_axis=2, concat_axis=0, tiled=True)
    order = [0, *Z_FAR]
    order = order + [k ^ Z_NEAR for k in order]
    cot = jnp.concatenate(
        [lax.dynamic_index_in_dim(spread, z ^ k, 0, False) for k in order], 0
    )

    ones = gather_y(w_one)
    x_a = gather_z(tokens)
    start = jnp.where(first_section, x_a, cot)
    part = jnp.stack([bf16(dot(start, w, ((1,), (0,)))) for w in ones], 0)
    sum_one = reduce_row(part, core)
    hidden_a = bf16(gelu(sum_one))
    twos = jnp.stack(gather_y(w_two), 0)

    def leave(acts):
        return bf16(dot(acts, twos, ((0, 2), (0, 2))))

    def enter(acts):
        return jnp.stack([bf16(dot(acts, twos[k], ((1,), (0,)))) for k in range(NY)], 0)

    out = scatter_z_across(leave(join_cores(hidden_a, core, 1)))
    x_b = gather_z(bf16(f32(tokens) + out))
    pre_b = reduce_row(enter(x_b), core)
    hidden_b = bf16(gelu(pre_b))
    grad_pre_b = bf16(gelu_grad(pre_b, sum_one))
    back = scatter_z_across(leave(join_cores(grad_pre_b, core, 1)))
    grad_a = gather_z(bf16(f32(cot[:shard]) + back))
    grad_hidden_a = reduce_row(enter(grad_a), core)
    grad_pre_a = bf16(gelu_grad(sum_one, grad_hidden_a))

    hidden = jnp.where(first_section, hidden_a, hidden_b)
    grad_pre = jnp.where(first_section, grad_pre_a, grad_pre_b)
    x = jnp.where(first_section, x_a, x_b)
    grad = jnp.where(first_section, grad_a, cot)

    def own_hidden(acts):
        pieces = [acts[0]] + [swap_col(acts[k], 0, k) for k in Y_STEPS]
        joined = join_cores(jnp.stack(pieces, 0), core, 1)
        return joined.reshape(-1, hidden_width)

    x_all = jnp.concatenate(gather_y(x), 0)
    grad_all = jnp.concatenate(gather_y(grad), 0)
    grad_down = dot(own_hidden(hidden), grad_all, ((0,), (0,)))
    grad_up = dot(x_all, own_hidden(grad_pre), ((0,), (0,)))
    return (grad_up[None], grad_down[None])


def solution(mesh):
    placed = (
        P("col", "row"),
        P("section", "row", "col"),
        P("section", "col", "row"),
        P("row", None),
    )
    return jax.shard_map(
        body,
        mesh=mesh,
        in_specs=placed,
        out_specs=(P("section", "row", "col"), P("section", "col", "row")),
        check_vma=False,
    )
```

```python
import jax
import jax.numpy as jnp
from jax import lax
from jax.sharding import PartitionSpec as P

NY = 4
NZ = 8
Z_NEAR = 1
Z_FAR = (2, 4, 6)
Y_STEPS = (1, 3, 2)
Y_GROUPS = [[z * NY + y for y in range(NY)] for z in range(NZ)]


def gelu(values):
    return jax.nn.gelu(values, approximate=True)


def gelu_grad(values, upstream):
    return jax.vjp(gelu, values)[1](upstream)[0]


def swap_col(value, dz, dy):
    pairs = []
    for z in range(NZ):
        for y in range(NY):
            pairs.append((z * NY + y, (z ^ dz) * NY + (y ^ dy)))
    return lax.ppermute(value, "col", pairs)


def swap_section(value, dz):
    cols = NZ * NY
    pairs = []
    for s in range(2):
        for z in range(NZ):
            for y in range(NY):
                pairs.append((s * cols + z * NY + y, (1 - s) * cols + (z ^ dz) * NY + y))
    return lax.ppermute(value, ("section", "col"), pairs)


def swap_row(value, by):
    return lax.ppermute(value, "row", [(r, r ^ by) for r in range(4)])


def dot(left, right, dims):
    return lax.dot_general(left, right, (dims, ((), ())), preferred_element_type=jnp.float32)


def bf16(values):
    return values.astype(jnp.bfloat16)


def f32(values):
    return values.astype(jnp.float32)


def after(value, *others):
    return lax.optimization_barrier((value, *others))


def gather_z(shard):
    near = jnp.concatenate([shard] + [swap_col(shard, k, 0) for k in Z_FAR], 0)
    return jnp.concatenate([near, swap_col(near, Z_NEAR, 0)], 0)


def gather_y(block, parts=1):
    cut = jnp.split(block, parts, 0)
    got = {0: block}
    for k in Y_STEPS:
        got[k] = jnp.concatenate([swap_col(piece, 0, k) for piece in cut], 0)
    return [got[k] for k in range(NY)]


def scatter_z_across(partial):
    half = partial.shape[0] // 2
    kept = bf16(f32(partial[:half]) + f32(swap_col(partial[half:], Z_NEAR, 0)))
    rows = half // 4
    total = f32(swap_section(kept[:rows], 0))
    for i, k in enumerate(Z_FAR):
        total = total + f32(swap_section(kept[(i + 1) * rows : (i + 2) * rows], k))
    return total


def chip_sum(partial, core):
    blocks, tokens, width = partial.shape
    halves = partial.reshape(blocks, 2, tokens // 2, width)
    mine = lax.dynamic_index_in_dim(halves, core, 1, False)
    other = lax.dynamic_index_in_dim(halves, 1 - core, 1, False)
    return f32(mine) + f32(swap_row(other, 1))


def reduce_row(partial, core):
    chip = chip_sum(partial, core)
    return chip + f32(swap_row(bf16(chip), 2))


def join_cores(mine, core, axis):
    other = swap_row(mine, 1)
    first = jnp.where(core == 0, mine, other)
    second = jnp.where(core == 0, other, mine)
    return jnp.concatenate([first, second], axis)


def body(tokens, w_up, w_down, cotangent):
    first_section = lax.axis_index("section") == 0
    row = lax.axis_index("row")
    core = row % 2
    col = lax.axis_index("col")
    y = col % NY
    shard, width = tokens.shape
    up = w_up[0]
    down = w_down[0]
    hidden_width = up.shape[1]

    ups = gather_y(up, 2)
    down_all = lax.all_gather(down, "col", axis=0, axis_index_groups=Y_GROUPS)

    held = cotangent.shape[0] // shard
    owner = col // held
    at = (col % held) * shard
    cot_shard = lax.dynamic_slice(cotangent, (at, row * width), (shard, width))
    for k in (1, 2, 3):
        piece = lax.dynamic_slice(cotangent, (at, (row ^ k) * width), (shard, width))
        cot_shard = jnp.where(row ^ owner == k, swap_row(piece, k), cot_shard)

    start = gather_z(jnp.where(first_section, tokens, cot_shard))

    def enter(acts, weights, dims):
        return jnp.stack([bf16(dot(acts, w, dims)) for w in weights], 0)

    def leave(acts, weights, dims):
        total = dot(acts[0], weights[0], dims)
        for k in range(1, NY):
            total = total + dot(acts[k], weights[k], dims)
        return bf16(total)

    ahead, back = ((1,), (0,)), ((1,), (1,))
    pre_a = reduce_row(enter(start, ups, ahead), core)
    hidden_a = bf16(gelu(pre_a))
    downs = [lax.dynamic_index_in_dim(down_all, y ^ k, 0, False) for k in range(NY)]
    out_part = leave(join_cores(hidden_a, core, 1), downs, ahead)
    grad_hidden_b = reduce_row(enter(start, downs, back), core)
    boundary = bf16(f32(tokens) + scatter_z_across(out_part))
    boundary, grad_hidden_b = after(boundary, grad_hidden_b)

    x_b = gather_z(boundary)
    x = jnp.where(first_section, start, x_b)
    xs = gather_y(x)
    pre_b = reduce_row(enter(x_b, ups, ahead), core)
    hidden_b = bf16(gelu(pre_b))
    grad_pre_b = bf16(gelu_grad(pre_b, grad_hidden_b))
    back_part = leave(join_cores(grad_pre_b, core, 1), ups, back)
    back_part, *xs = after(back_part, *xs)
    hidden = jnp.where(first_section, hidden_a, hidden_b)

    def own_hidden(acts):
        got = {0: acts[0]}
        for k in Y_STEPS:
            got[k] = swap_col(acts[k], 0, k)
        joined = join_cores(jnp.stack([got[k] for k in range(NY)], 0), core, 1)
        return joined.reshape(-1, hidden_width)

    hidden_all = own_hidden(hidden)
    grad_boundary = bf16(f32(cot_shard) + scatter_z_across(back_part))
    grad_boundary, hidden_all = after(grad_boundary, hidden_all)
    grad_a = gather_z(grad_boundary)
    grad = jnp.where(first_section, grad_a, start)
    grads = gather_y(grad)
    grad_hidden_a = reduce_row(enter(grad_a, downs, back), core)
    grad_pre_a = bf16(gelu_grad(pre_a, grad_hidden_a))
    grad_pre = jnp.where(first_section, grad_pre_a, grad_pre_b)
    grad_pre, *grads = after(grad_pre, *grads)

    x_all = jnp.concatenate(xs, 0)
    grad_all = jnp.concatenate(grads, 0)
    grad_down = dot(hidden_all, grad_all, ((0,), (0,)))
    grad_up = dot(x_all, own_hidden(grad_pre), ((0,), (0,)))
    return (grad_up[None], grad_down[None])


def solution(mesh):
    placed = (
        P("col", "row"),
        P("section", "row", "col"),
        P("section", "col", "row"),
        P("row", None),
    )
    return jax.shard_map(
        body,
        mesh=mesh,
        in_specs=placed,
        out_specs=(P("section", "row", "col"), P("section", "col", "row")),
        check_vma=False,
    )
```

```python
import jax
import jax.numpy as jnp
from jax import lax
from jax.sharding import PartitionSpec as P

NY = 4
NZ = 8
Z_NEAR = 1
Z_FAR = (2, 4, 6)
Y_STEPS = (1, 3, 2)
Y_GROUPS = [[z * NY + y for y in range(NY)] for z in range(NZ)]


def gelu(values):
    return jax.nn.gelu(values, approximate=True)


def gelu_grad(values, upstream):
    return jax.vjp(gelu, values)[1](upstream)[0]


def swap_col(value, dz, dy):
    pairs = []
    for z in range(NZ):
        for y in range(NY):
            pairs.append((z * NY + y, (z ^ dz) * NY + (y ^ dy)))
    return lax.ppermute(value, "col", pairs)


def swap_section(value, dz):
    cols = NZ * NY
    pairs = []
    for s in range(2):
        for z in range(NZ):
            for y in range(NY):
                pairs.append((s * cols + z * NY + y, (1 - s) * cols + (z ^ dz) * NY + y))
    return lax.ppermute(value, ("section", "col"), pairs)


def swap_row(value, by):
    return lax.ppermute(value, "row", [(r, r ^ by) for r in range(4)])


def dot(left, right, dims):
    return lax.dot_general(left, right, (dims, ((), ())), preferred_element_type=jnp.float32)


def bf16(values):
    return values.astype(jnp.bfloat16)


def f32(values):
    return values.astype(jnp.float32)


def after(value, *others):
    return lax.optimization_barrier((value, *others))


def gather_z(shard):
    near = jnp.concatenate([shard] + [swap_col(shard, k, 0) for k in Z_FAR], 0)
    return jnp.concatenate([near, swap_col(near, Z_NEAR, 0)], 0)


def gather_y(block, parts=1):
    cut = jnp.split(block, parts, 0)
    got = {0: block}
    for k in Y_STEPS:
        got[k] = jnp.concatenate([swap_col(piece, 0, k) for piece in cut], 0)
    return [got[k] for k in range(NY)]


def scatter_z_across(partial):
    half = partial.shape[0] // 2
    kept = bf16(f32(partial[:half]) + f32(swap_col(partial[half:], Z_NEAR, 0)))
    rows = half // 4
    total = f32(swap_section(kept[:rows], 0))
    for i, k in enumerate(Z_FAR):
        total = total + f32(swap_section(kept[(i + 1) * rows : (i + 2) * rows], k))
    return total


def chip_sum(partial, core):
    blocks, tokens, width = partial.shape
    halves = partial.reshape(blocks, 2, tokens // 2, width)
    mine = lax.dynamic_index_in_dim(halves, core, 1, False)
    other = lax.dynamic_index_in_dim(halves, 1 - core, 1, False)
    return f32(mine) + f32(swap_row(other, 1))


def reduce_row(partial, core):
    chip = chip_sum(partial, core)
    return chip + f32(swap_row(bf16(chip), 2))


def join_cores(mine, core, axis):
    other = swap_row(mine, 1)
    first = jnp.where(core == 0, mine, other)
    second = jnp.where(core == 0, other, mine)
    return jnp.concatenate([first, second], axis)


def body(tokens, w_up, w_down, cotangent):
    first_section = lax.axis_index("section") == 0
    row = lax.axis_index("row")
    core = row % 2
    col = lax.axis_index("col")
    y = col % NY
    shard, width = tokens.shape
    up = w_up[0]
    down = w_down[0]
    hidden_width = up.shape[1]

    def whole_group(block):
        got = lax.all_gather(block, "col", axis=0, axis_index_groups=Y_GROUPS)
        return [lax.dynamic_index_in_dim(got, y ^ k, 0, False) for k in range(NY)]

    held = cotangent.shape[0] // shard
    owner = col // held
    at = (col % held) * shard
    cot_shard = lax.dynamic_slice(cotangent, (at, row * width), (shard, width))
    for k in (1, 2, 3):
        piece = lax.dynamic_slice(cotangent, (at, (row ^ k) * width), (shard, width))
        cot_shard = jnp.where(row ^ owner == k, swap_row(piece, k), cot_shard)

    ahead, back = ((1,), (0,)), ((1,), (1,))

    def enter(acts, weights, dims):
        return jnp.stack([bf16(dot(a, w, dims)) for a, w in zip(acts, weights)], 0)

    def leave(acts, weights, dims):
        total = dot(acts[0], weights[0], dims)
        for k in range(1, NY):
            total = total + dot(acts[k], weights[k], dims)
        return bf16(total)

    def exchange_y(acts):
        got = {0: acts[0]}
        for k in Y_STEPS:
            got[k] = swap_col(acts[k], 0, k)
        return jnp.stack([got[k] for k in range(NY)], 0)

    x_a = gather_z(tokens)
    pre_a = reduce_row(enter(gather_y(x_a), [up] * NY, ahead), core)
    hidden_a = bf16(gelu(pre_a))
    downs = whole_group(down)
    out_part = leave(join_cores(exchange_y(hidden_a), core, 1), downs, ahead)
    boundary = bf16(f32(tokens) + scatter_z_across(out_part))

    ups = whole_group(up)
    cot = gather_z(cot_shard)
    grad_hidden_b = reduce_row(enter([cot] * NY, downs, back), core)
    x_b = gather_z(boundary)
    x = jnp.where(first_section, x_a, x_b)
    xs = whole_group(x)
    part_b = enter([x_b] * NY, ups, ahead)
    part_b, grad_hidden_b = after(part_b, grad_hidden_b)
    pre_b = reduce_row(part_b, core)
    hidden_b = bf16(gelu(pre_b))
    grad_pre_b = bf16(gelu_grad(pre_b, grad_hidden_b))
    back_part = leave(join_cores(grad_pre_b, core, 1), ups, back)
    hidden = jnp.where(first_section, hidden_a, exchange_y(hidden_b))
    hidden_all = join_cores(hidden, core, 1).reshape(-1, hidden_width)
    grad_boundary = bf16(f32(cot_shard) + scatter_z_across(back_part))
    grad_boundary, hidden_all = after(grad_boundary, hidden_all)

    grad_a = gather_z(grad_boundary)
    grad = jnp.where(first_section, grad_a, cot)
    grads = gather_y(grad)
    grad_hidden_a = bf16(reduce_row(enter([grad_a] * NY, downs, back), core))
    moved = exchange_y(jnp.where(first_section, grad_hidden_a, grad_pre_b))
    moved, *grads = after(moved, *grads)
    grad_pre_a = bf16(gelu_grad(pre_a, f32(moved)))
    grad_pre = jnp.where(first_section, grad_pre_a, moved)
    grad_pre_all = join_cores(grad_pre, core, 1).reshape(-1, hidden_width)

    x_all = jnp.concatenate(xs, 0)
    grad_all = jnp.concatenate(grads, 0)
    grad_down = dot(hidden_all, grad_all, ((0,), (0,)))
    grad_up = dot(x_all, grad_pre_all, ((0,), (0,)))
    return (grad_up[None], grad_down[None])


def solution(mesh):
    placed = (
        P("col", "row"),
        P("section", "row", "col"),
        P("section", "col", "row"),
        P("row", None),
    )
    return jax.shard_map(
        body,
        mesh=mesh,
        in_specs=placed,
        out_specs=(P("section", "row", "col"), P("section", "col", "row")),
        check_vma=False,
    )
```

```python
import jax
import jax.numpy as jnp
from jax import lax
from jax.experimental import pallas as pl
from jax.experimental.pallas import tpu as pltpu
from jax.sharding import PartitionSpec as P

NY = 4
NZ = 8
Z_NEAR = 1
Z_FAR = (2, 4, 6)
Y_STEPS = (1, 3, 2)


def gelu(values):
    return jax.nn.gelu(values, approximate=True)


def gelu_grad(values, upstream):
    return jax.vjp(gelu, values)[1](upstream)[0]


def swap_col(value, dz, dy):
    pairs = []
    for z in range(NZ):
        for y in range(NY):
            pairs.append((z * NY + y, (z ^ dz) * NY + (y ^ dy)))
    return lax.ppermute(value, "col", pairs)


def swap_section(value, dz):
    cols = NZ * NY
    pairs = []
    for s in range(2):
        for z in range(NZ):
            for y in range(NY):
                pairs.append((s * cols + z * NY + y, (1 - s) * cols + (z ^ dz) * NY + y))
    return lax.ppermute(value, ("section", "col"), pairs)


def swap_row(value, by):
    return lax.ppermute(value, "row", [(r, r ^ by) for r in range(4)])


def dot(left, right, dims):
    return lax.dot_general(left, right, (dims, ((), ())), preferred_element_type=jnp.float32)


def bf16(values):
    return values.astype(jnp.bfloat16)


def f32(values):
    return values.astype(jnp.float32)


def after(value, *others):
    return lax.optimization_barrier((value, *others))


def gather_z(shard):
    near = jnp.concatenate([shard] + [swap_col(shard, k, 0) for k in Z_FAR], 0)
    return jnp.concatenate([near, swap_col(near, Z_NEAR, 0)], 0)


def swap_y(blocks, own):
    got = {0: own}
    for k in Y_STEPS:
        got[k] = swap_col(blocks[k], 0, k)
    return [got[k] for k in range(NY)]


def scatter_z_across(partial):
    half = partial.shape[0] // 2
    kept = bf16(f32(partial[:half]) + f32(swap_col(partial[half:], Z_NEAR, 0)))
    rows = half // 4
    total = f32(swap_section(kept[:rows], 0))
    for i, k in enumerate(Z_FAR):
        total = total + f32(swap_section(kept[(i + 1) * rows : (i + 2) * rows], k))
    return total


def spread_cotangent(value, section):
    rows, per = 4, NZ * NY // 4
    pairs = []
    for a in range(rows):
        for b in range(rows):
            for i in range(per):
                source = (section * rows + a) * NZ * NY + b * per + i
                target = (section * rows + b) * NZ * NY + a * per + i
                pairs.append((source, target))
    return lax.ppermute(value, ("section", "row", "col"), pairs)


def chip_sum(partial, core):
    blocks, tokens, width = partial.shape
    halves = partial.reshape(blocks, 2, tokens // 2, width)
    mine = lax.dynamic_index_in_dim(halves, core, 1, False)
    other = lax.dynamic_index_in_dim(halves, 1 - core, 1, False)
    return f32(mine) + f32(swap_row(other, 1))


def reduce_row(partial, core):
    chip = chip_sum(partial, core)
    return chip + f32(swap_row(bf16(chip), 2))


def join_cores(mine, core, axis):
    other = swap_row(mine, 1)
    first = jnp.where(core == 0, mine, other)
    second = jnp.where(core == 0, other, mine)
    return jnp.concatenate([first, second], axis)


def choose_kernel(flag_ref, plain_ref, other_ref, out_ref):
    @pl.when(flag_ref[0] == 1)
    def _():
        out_ref[...] = plain_ref[...]

    @pl.when(flag_ref[0] == 0)
    def _():
        out_ref[...] = other_ref[...].T


def choose(flag, plain, other):
    whole = pl.BlockSpec(memory_space=pltpu.VMEM)
    return pl.pallas_call(
        choose_kernel,
        out_shape=jax.ShapeDtypeStruct(plain.shape, plain.dtype),
        in_specs=[pl.BlockSpec(memory_space=pltpu.SMEM), whole, whole],
        out_specs=whole,
        compiler_params=pltpu.CompilerParams(vmem_limit_bytes=32 * 2**20),
        cost_estimate=pl.CostEstimate(
            flops=0, bytes_accessed=6 * plain.size, transcendentals=0
        ),
        name="choose",
    )(flag, plain, other)


def body(tokens, w_up, w_down, cotangent):
    first_section = lax.axis_index("section") == 0
    core = lax.axis_index("row") % 2
    col = lax.axis_index("col")
    shard, width = tokens.shape
    up = w_up[0]
    down = w_down[0]
    hidden_width = up.shape[1]

    def pick(in_a, in_b):
        return jnp.where(first_section, in_a, in_b)

    held = cotangent.shape[0] // shard
    piece = lax.dynamic_slice(
        cotangent, ((col % held) * shard, (col // held) * width), (shard, width)
    )
    cot_b = spread_cotangent(piece, 1)
    cot_a = spread_cotangent(piece, 0)

    flag = jnp.where(first_section, 1, 0).astype(jnp.int32).reshape(1)
    w_share = choose(flag, down, up)
    w_own = choose(flag, up, down)
    shares = {0: w_share}
    for k in (1, 3):
        shares[k] = swap_col(w_share, 0, k)

    ahead, back = ((1,), (0,)), ((1,), (1,))

    def enter(acts, weights, dims):
        return jnp.stack([bf16(dot(a, w, dims)) for a, w in zip(acts, weights)], 0)

    def leave(acts):
        total = dot(acts[0], shares[0], ahead)
        for k in range(1, NY):
            total = total + dot(acts[k], shares[k], ahead)
        return bf16(total)

    def exchange_y(acts):
        return jnp.stack(swap_y(acts, acts[0]), 0)

    start = gather_z(pick(tokens, cot_b))
    start, shares[1], shares[3] = after(start, shares[1], shares[3])
    starts = swap_y([start] * NY, start)
    part = enter(starts, [w_own] * NY, ahead)
    part, w_share = after(part, w_share)
    shares[2] = swap_col(w_share, 0, 2)
    sum_one = reduce_row(part, core)
    hidden_a = bf16(gelu(sum_one))
    act_one = pick(hidden_a, bf16(sum_one))
    act_one, shares[2] = after(act_one, shares[2])
    moved = exchange_y(act_one)

    out_part = leave(join_cores(moved, core, 1))
    boundary = bf16(f32(tokens) + scatter_z_across(out_part))
    x_b = gather_z(boundary)
    weights = [shares[k] for k in range(NY)]
    pre_b = reduce_row(enter([x_b] * NY, weights, back), core)
    hidden_b = bf16(gelu(pre_b))
    grad_pre_b = bf16(gelu_grad(pre_b, f32(moved)))
    back_part = leave(join_cores(grad_pre_b, core, 1))
    back_part, hidden_b = after(back_part, hidden_b)
    hidden = pick(hidden_a, exchange_y(hidden_b))
    hidden_all = join_cores(hidden, core, 1).reshape(-1, hidden_width)
    grad_boundary = bf16(f32(cot_a) + scatter_z_across(back_part))
    grad_boundary, hidden_all = after(grad_boundary, hidden_all)

    grad_a = gather_z(grad_boundary)
    second = pick(grad_a, x_b)
    seconds = swap_y([second] * NY, second)
    grad_hidden_a = reduce_row(enter([grad_a] * NY, weights, back), core)
    last = exchange_y(pick(bf16(grad_hidden_a), grad_pre_b))
    last, *seconds = after(last, *seconds)
    grad_pre = pick(bf16(gelu_grad(sum_one, f32(last))), last)
    grad_pre_all = join_cores(grad_pre, core, 1).reshape(-1, hidden_width)

    x_all = jnp.concatenate([pick(a, b) for a, b in zip(starts, seconds)], 0)
    grad_all = jnp.concatenate([pick(b, a) for a, b in zip(starts, seconds)], 0)
    grad_down = dot(hidden_all, grad_all, ((0,), (0,)))
    grad_up = dot(x_all, grad_pre_all, ((0,), (0,)))
    return (grad_up[None], grad_down[None])


def solution(mesh):
    placed = (
        P("col", "row"),
        P("section", "row", "col"),
        P("section", "col", "row"),
        P("row", None),
    )
    return jax.shard_map(
        body,
        mesh=mesh,
        in_specs=placed,
        out_specs=(P("section", "row", "col"), P("section", "col", "row")),
        check_vma=False,
    )
```

```python
import jax
import jax.numpy as jnp
from jax import lax
from jax.experimental import pallas as pl
from jax.experimental.pallas import tpu as pltpu
from jax.sharding import PartitionSpec as P

NY = 4
NZ = 8
Z_ORDER = (0, 2, 6, 4, 1, 3, 7, 5)
Y_STEPS = (1, 3, 2)


def gelu(values):
    return jax.nn.gelu(values, approximate=True)


def gelu_grad(values, upstream):
    return jax.vjp(gelu, values)[1](upstream)[0]


def swap_col(value, dz, dy):
    pairs = []
    for z in range(NZ):
        for y in range(NY):
            pairs.append((z * NY + y, (z ^ dz) * NY + (y ^ dy)))
    return lax.ppermute(value, "col", pairs)


def swap_section(value, dz):
    cols = NZ * NY
    pairs = []
    for s in range(2):
        for z in range(NZ):
            for y in range(NY):
                pairs.append((s * cols + z * NY + y, (1 - s) * cols + (z ^ dz) * NY + y))
    return lax.ppermute(value, ("section", "col"), pairs)


def swap_row(value, by):
    return lax.ppermute(value, "row", [(r, r ^ by) for r in range(4)])


def dot(left, right, dims):
    return lax.dot_general(left, right, (dims, ((), ())), preferred_element_type=jnp.float32)


def bf16(values):
    return values.astype(jnp.bfloat16)


def f32(values):
    return values.astype(jnp.float32)


def after(value, *others):
    return lax.optimization_barrier((value, *others))


def gather_z(shard):
    two = jnp.concatenate([shard, swap_col(shard, 2, 0)], 0)
    four = jnp.concatenate([two, swap_col(two, 6, 0)], 0)
    return jnp.concatenate([four, swap_col(four, 1, 0)], 0)


def swap_y(blocks, own):
    got = {0: own}
    for k in Y_STEPS:
        got[k] = swap_col(blocks[k], 0, k)
    return [got[k] for k in range(NY)]


def forward_y(one, three):
    half = one.shape[0] // 2
    return jnp.concatenate([swap_col(three[:half], 0, 1), swap_col(one[half:], 0, 3)], 0)


def halve(partial, dz):
    half = partial.shape[0] // 2
    return bf16(f32(partial[:half]) + f32(swap_col(partial[half:], dz, 0)))


def finish_across(partial):
    two = halve(partial, 6)
    rows = two.shape[0] // 2
    return f32(swap_section(two[:rows], 0)) + f32(swap_section(two[rows:], 2))


def chip_sum(partial, core):
    blocks, tokens, width = partial.shape
    halves = partial.reshape(blocks, 2, tokens // 2, width)
    mine = lax.dynamic_index_in_dim(halves, core, 1, False)
    other = lax.dynamic_index_in_dim(halves, 1 - core, 1, False)
    return f32(mine) + f32(swap_row(other, 1))


def reduce_row(partial, core):
    chip = chip_sum(partial, core)
    return chip + f32(swap_row(bf16(chip), 2))


def join_cores(mine, core, axis):
    other = swap_row(mine, 1)
    first = jnp.where(core == 0, mine, other)
    second = jnp.where(core == 0, other, mine)
    return jnp.concatenate([first, second], axis)


def choose_kernel(flag_ref, plain_ref, other_ref, out_ref):
    @pl.when(flag_ref[0] == 1)
    def _():
        out_ref[...] = plain_ref[...]

    @pl.when(flag_ref[0] == 0)
    def _():
        out_ref[...] = other_ref[...].T


def choose(flag, plain, other):
    whole = pl.BlockSpec(memory_space=pltpu.VMEM)
    return pl.pallas_call(
        choose_kernel,
        out_shape=jax.ShapeDtypeStruct(plain.shape, plain.dtype),
        in_specs=[pl.BlockSpec(memory_space=pltpu.SMEM), whole, whole],
        out_specs=whole,
        compiler_params=pltpu.CompilerParams(vmem_limit_bytes=32 * 2**20),
        cost_estimate=pl.CostEstimate(
            flops=0, bytes_accessed=6 * plain.size, transcendentals=0
        ),
        name="choose",
    )(flag, plain, other)


def begin_kernel(where_ref, gathered_ref, *refs):
    *held, start_ref, shard_ref = refs
    row, z = where_ref[1], where_ref[2]
    rows = shard_ref.shape[0]

    @pl.when(where_ref[0] == 1)
    def _():
        start_ref[...] = gathered_ref[...]

    for j in range(4):
        owner = row ^ j

        @pl.when(where_ref[0] == 0)
        def _():
            for i in range(2):
                offset = (2 * owner + i) ^ z
                pair = offset // 2
                at = (offset % 2) * 4 + (pair ^ (pair // 2))
                at = pl.multiple_of(at * rows, rows)
                start_ref[pl.ds(at, rows), :] = held[j][i * rows : (i + 1) * rows, :]

        @pl.when(owner == z // 2)
        def _():
            at = pl.multiple_of((z % 2) * rows, rows)
            shard_ref[...] = held[j][pl.ds(at, rows), :]


def begin(where, gathered, held):
    whole = pl.BlockSpec(memory_space=pltpu.VMEM)
    rows = held[0].shape[0] // 2
    return pl.pallas_call(
        begin_kernel,
        out_shape=[
            jax.ShapeDtypeStruct(gathered.shape, gathered.dtype),
            jax.ShapeDtypeStruct((rows, gathered.shape[1]), gathered.dtype),
        ],
        in_specs=[pl.BlockSpec(memory_space=pltpu.SMEM)] + [whole] * 5,
        out_specs=[whole] * 2,
        compiler_params=pltpu.CompilerParams(vmem_limit_bytes=32 * 2**20),
        cost_estimate=pl.CostEstimate(
            flops=0, bytes_accessed=6 * gathered.size, transcendentals=0
        ),
        name="begin",
    )(where, gathered, *held)


def body(tokens, w_up, w_down, cotangent):
    first_section = lax.axis_index("section") == 0
    core = lax.axis_index("row") % 2
    col = lax.axis_index("col")
    shard, width = tokens.shape
    up = w_up[0]
    down = w_down[0]
    hidden_width = up.shape[1]

    def pick(in_a, in_b):
        return jnp.where(first_section, in_a, in_b)

    row = lax.axis_index("row")
    z, y = col // NY, col % NY
    blocks = cotangent.reshape(-1, NY, shard, cotangent.shape[1])
    held = []
    for k in range(4):
        mine = lax.dynamic_slice(
            blocks, (0, y, 0, (row ^ k) * width), (blocks.shape[0], 1, shard, width)
        ).reshape(-1, width)
        held.append(swap_row(mine, k) if k else mine)

    flag = jnp.where(first_section, 1, 0).astype(jnp.int32).reshape(1)
    w_share = choose(flag, down, up)
    w_own = choose(flag, up, down)
    shares = {0: w_share}
    for k in (1, 3):
        shares[k] = swap_col(w_share, 0, k)

    ahead, back = ((1,), (0,)), ((1,), (1,))

    def enter(acts, weights, dims):
        return jnp.stack([bf16(dot(a, w, dims)) for a, w in zip(acts, weights)], 0)

    def leave(acts):
        total = dot(acts[0], shares[0], ahead)
        for k in range(1, NY):
            total = total + dot(acts[k], shares[k], ahead)
        return bf16(total)

    def exchange_y(acts):
        return jnp.stack(swap_y(acts, acts[0]), 0)

    gathered = gather_z(tokens)
    where = jnp.stack([flag[0], row, z]).astype(jnp.int32)
    start, cot_shard = begin(where, gathered, held)
    start, shares[1], shares[3] = after(start, shares[1], shares[3])
    starts = swap_y([start] * NY, start)
    part = enter(starts, [w_own] * NY, ahead)
    part, one, three = after(part, shares[1], shares[3])
    far = forward_y(one, three)
    sum_one = reduce_row(part, core)
    hidden_a = bf16(gelu(sum_one))
    act_one = pick(hidden_a, bf16(sum_one))
    act_one, shares[2] = after(act_one, far)
    moved = exchange_y(act_one)

    out_part = leave(join_cores(moved, core, 1))
    boundary = bf16(f32(tokens) + finish_across(halve(out_part, 1)))
    x_b = gather_z(boundary)
    weights = [shares[k] for k in range(NY)]
    pre_b = reduce_row(enter([x_b] * NY, weights, back), core)
    hidden_b = bf16(gelu(pre_b))
    grad_pre_b = bf16(gelu_grad(pre_b, f32(moved)))
    back_part = halve(leave(join_cores(grad_pre_b, core, 1)), 1)
    back_part, hidden_b = after(back_part, hidden_b)
    hidden = pick(hidden_a, exchange_y(hidden_b))
    hidden_all = join_cores(hidden, core, 1).reshape(-1, hidden_width)
    grad_boundary = bf16(f32(cot_shard) + finish_across(back_part))

    grad_a = gather_z(grad_boundary)
    second = pick(grad_a, x_b)
    seconds = {0: second, 1: swap_col(second, 0, 1), 3: swap_col(second, 0, 3)}
    part = enter([grad_a] * NY, weights, back)
    part, hidden_all = after(part, hidden_all)
    grad_hidden_a = reduce_row(part, core)
    last = pick(bf16(grad_hidden_a), grad_pre_b)
    last, seconds[1], seconds[3] = after(last, seconds[1], seconds[3])
    last = exchange_y(last)
    seconds[2] = forward_y(seconds[1], seconds[3])
    seconds = [seconds[k] for k in range(NY)]
    grad_pre = pick(bf16(gelu_grad(sum_one, f32(last))), last)
    grad_pre_all = join_cores(grad_pre, core, 1).reshape(-1, hidden_width)

    x_all = jnp.concatenate([pick(a, b) for a, b in zip(starts, seconds)], 0)
    grad_all = jnp.concatenate([pick(b, a) for a, b in zip(starts, seconds)], 0)
    grad_down = dot(hidden_all, grad_all, ((0,), (0,)))
    grad_up = dot(x_all, grad_pre_all, ((0,), (0,)))
    return (grad_up[None], grad_down[None])


def solution(mesh):
    placed = (
        P("col", "row"),
        P("section", "row", "col"),
        P("section", "col", "row"),
        P("row", None),
    )
    return jax.shard_map(
        body,
        mesh=mesh,
        in_specs=placed,
        out_specs=(P("section", "row", "col"), P("section", "col", "row")),
        check_vma=False,
    )
```

```python
import jax
import jax.numpy as jnp
from jax import lax
from jax.experimental import pallas as pl
from jax.experimental.pallas import tpu as pltpu
from jax.sharding import PartitionSpec as P

NY = 4
NZ = 8
Z_PAIRS = (6, 1, 7)
Y_STEPS = (1, 3, 2)


def gelu(values):
    return jax.nn.gelu(values, approximate=True)


def gelu_grad(values, upstream):
    return jax.vjp(gelu, values)[1](upstream)[0]


def swap_col(value, dz, dy):
    pairs = []
    for z in range(NZ):
        for y in range(NY):
            pairs.append((z * NY + y, (z ^ dz) * NY + (y ^ dy)))
    return lax.ppermute(value, "col", pairs)


def swap_section(value, dz):
    cols = NZ * NY
    pairs = []
    for s in range(2):
        for z in range(NZ):
            for y in range(NY):
                pairs.append((s * cols + z * NY + y, (1 - s) * cols + (z ^ dz) * NY + y))
    return lax.ppermute(value, ("section", "col"), pairs)


def swap_row(value, by):
    return lax.ppermute(value, "row", [(r, r ^ by) for r in range(4)])


def dot(left, right, dims):
    return lax.dot_general(left, right, (dims, ((), ())), preferred_element_type=jnp.float32)


def bf16(values):
    return values.astype(jnp.bfloat16)


def f32(values):
    return values.astype(jnp.float32)


def after(value, *others):
    return lax.optimization_barrier((value, *others))


def gather_pairs(pair):
    return jnp.concatenate([pair] + [swap_col(pair, k, 0) for k in Z_PAIRS], 0)


def swap_y(blocks, own):
    got = {0: own}
    for k in Y_STEPS:
        got[k] = swap_col(blocks[k], 0, k)
    return [got[k] for k in range(NY)]


def forward_y(one, three):
    half = one.shape[0] // 2
    return jnp.concatenate([swap_col(three[:half], 0, 1), swap_col(one[half:], 0, 3)], 0)


def sum_pairs(partial):
    rows = partial.shape[0] // 4
    total = f32(partial[:rows])
    for i, k in enumerate(Z_PAIRS):
        at = (i + 1) * rows
        total = total + f32(swap_col(partial[at : at + rows], k, 0))
    return bf16(total)


def cross(pair):
    half = pair.shape[0] // 2
    turned = jnp.concatenate([pair[half:], pair[:half]], 0)
    return f32(swap_section(pair, 0)) + f32(swap_section(turned, 2))


def reduce_row(partial, core, axis):
    shape = partial.shape
    halves = partial.reshape(*shape[:axis], 2, shape[axis] // 2, *shape[axis + 1 :])
    mine = lax.dynamic_index_in_dim(halves, core, axis, False)
    other = lax.dynamic_index_in_dim(halves, 1 - core, axis, False)
    chip = f32(mine) + f32(swap_row(other, 1))
    return chip + f32(swap_row(bf16(chip), 2))


def join_cores(mine, core, axis):
    other = swap_row(mine, 1)
    first = jnp.where(core == 0, mine, other)
    second = jnp.where(core == 0, other, mine)
    return jnp.concatenate([first, second], axis)


def choose_kernel(flag_ref, plain_ref, other_ref, out_ref):
    @pl.when(flag_ref[0] == 1)
    def _():
        out_ref[...] = plain_ref[...]

    @pl.when(flag_ref[0] == 0)
    def _():
        out_ref[...] = other_ref[...].T


def choose(flag, plain, other):
    whole = pl.BlockSpec(memory_space=pltpu.VMEM)
    return pl.pallas_call(
        choose_kernel,
        out_shape=jax.ShapeDtypeStruct(plain.shape, plain.dtype),
        in_specs=[pl.BlockSpec(memory_space=pltpu.SMEM), whole, whole],
        out_specs=whole,
        compiler_params=pltpu.CompilerParams(vmem_limit_bytes=32 * 2**20),
        cost_estimate=pl.CostEstimate(
            flops=0, bytes_accessed=6 * plain.size, transcendentals=0
        ),
        name="choose",
    )(flag, plain, other)


def begin_kernel(where_ref, gathered_ref, *refs):
    *held, start_ref, pair_ref = refs
    row, z = where_ref[1], where_ref[2]
    rows = pair_ref.shape[0] // 2

    @pl.when(where_ref[0] == 1)
    def _():
        start_ref[...] = gathered_ref[...]

    for j in range(4):
        owner = row ^ j
        for i in range(2):
            offset = (2 * owner + i) ^ z
            group = offset // 2
            at = (offset % 2) * 4 + (group ^ (group // 2))
            at = pl.multiple_of(at * rows, rows)

            @pl.when(where_ref[0] == 0)
            def _():
                start_ref[pl.ds(at, rows), :] = held[j][i * rows : (i + 1) * rows, :]

            @pl.when(offset == 0)
            def _():
                pair_ref[0:rows, :] = held[j][i * rows : (i + 1) * rows, :]

            @pl.when(offset == 2)
            def _():
                pair_ref[rows:, :] = held[j][i * rows : (i + 1) * rows, :]


def begin(where, gathered, held):
    whole = pl.BlockSpec(memory_space=pltpu.VMEM)
    rows = held[0].shape[0]
    return pl.pallas_call(
        begin_kernel,
        out_shape=[
            jax.ShapeDtypeStruct(gathered.shape, gathered.dtype),
            jax.ShapeDtypeStruct((rows, gathered.shape[1]), gathered.dtype),
        ],
        in_specs=[pl.BlockSpec(memory_space=pltpu.SMEM)] + [whole] * 5,
        out_specs=[whole] * 2,
        compiler_params=pltpu.CompilerParams(vmem_limit_bytes=32 * 2**20),
        cost_estimate=pl.CostEstimate(
            flops=0, bytes_accessed=6 * gathered.size, transcendentals=0
        ),
        name="begin",
    )(where, gathered, *held)


def body(tokens, w_up, w_down, cotangent):
    first_section = lax.axis_index("section") == 0
    core = lax.axis_index("row") % 2
    col = lax.axis_index("col")
    shard, width = tokens.shape
    up = w_up[0]
    down = w_down[0]
    hidden_width = up.shape[1]

    def pick(in_a, in_b):
        return jnp.where(first_section, in_a, in_b)

    row = lax.axis_index("row")
    z, y = col // NY, col % NY
    blocks = cotangent.reshape(-1, NY, shard, cotangent.shape[1])
    held = []
    for k in range(4):
        mine = lax.dynamic_slice(
            blocks, (0, y, 0, (row ^ k) * width), (blocks.shape[0], 1, shard, width)
        ).reshape(-1, width)
        held.append(swap_row(mine, k) if k else mine)

    pair = jnp.concatenate([tokens, swap_col(tokens, 2, 0)], 0)

    flag = jnp.where(first_section, 1, 0).astype(jnp.int32)
    pair, flag_late = after(pair, flag)
    w_share = choose(flag_late.reshape(1), down, up)
    w_own = choose(flag.reshape(1), up, down)
    shares = {0: w_share}
    for k in (1, 3):
        shares[k] = swap_col(w_share, 0, k)

    ahead, back = ((1,), (0,)), ((1,), (1,))

    def blocks_of(acts):
        return [acts[:, k * hidden_width : (k + 1) * hidden_width] for k in range(NY)]

    def exchange_y(acts):
        return swap_y(acts, acts[0])

    gathered = gather_pairs(pair)
    where = jnp.stack([flag, row, z]).astype(jnp.int32)
    start, cot_pair = begin(where, gathered, held)
    start, shares[1], shares[3] = after(start, shares[1], shares[3])
    starts = swap_y([start] * NY, start)
    part = jnp.stack([bf16(dot(tok, w_own, ahead)) for tok in starts], 0)
    part, one, three = after(part, shares[1], shares[3])
    far = forward_y(one, three)
    sum_one = reduce_row(part, core, 1)
    hidden_a = bf16(gelu(sum_one))
    act_one = pick(hidden_a, bf16(sum_one))
    act_one, shares[2] = after(act_one, far)
    moved = jnp.concatenate(exchange_y(act_one), 1)
    weights = jnp.concatenate([shares[k] for k in range(NY)], 0)

    def enter(acts):
        return reduce_row(bf16(dot(acts, weights, back)), core, 0)

    def leave(acts):
        return sum_pairs(bf16(dot(join_cores(acts, core, 0), weights, ahead)))

    x_b = gather_pairs(bf16(f32(pair) + cross(leave(moved))))
    pre_b = enter(x_b)
    hidden_b = bf16(gelu(pre_b))
    grad_pre_b = bf16(gelu_grad(pre_b, f32(moved)))
    back_part = leave(grad_pre_b)
    back_part, hidden_b = after(back_part, hidden_b)
    hidden = pick(hidden_a, jnp.stack(exchange_y(blocks_of(hidden_b)), 0))
    hidden_all = join_cores(hidden, core, 1).reshape(-1, hidden_width)

    grad_a = gather_pairs(bf16(f32(cot_pair) + cross(back_part)))
    second = pick(grad_a, x_b)
    seconds = {0: second, 1: swap_col(second, 0, 1), 3: swap_col(second, 0, 3)}
    seconds[2] = forward_y(seconds[1], seconds[3])
    grad_a, hidden_all = after(grad_a, hidden_all)
    last = pick(bf16(enter(grad_a)), grad_pre_b)
    last, *seconds = after(last, *[seconds[k] for k in range(NY)])
    last = jnp.stack(exchange_y(blocks_of(last)), 0)
    grad_pre = pick(bf16(gelu_grad(sum_one, f32(last))), last)
    grad_pre_all = join_cores(grad_pre, core, 1).reshape(-1, hidden_width)

    x_all = jnp.concatenate([pick(a, b) for a, b in zip(starts, seconds)], 0)
    grad_all = jnp.concatenate([pick(b, a) for a, b in zip(starts, seconds)], 0)
    grad_down = dot(hidden_all, grad_all, ((0,), (0,)))
    grad_up = dot(x_all, grad_pre_all, ((0,), (0,)))
    return (grad_up[None], grad_down[None])


def solution(mesh):
    placed = (
        P("col", "row"),
        P("section", "row", "col"),
        P("section", "col", "row"),
        P("row", None),
    )
    return jax.shard_map(
        body,
        mesh=mesh,
        in_specs=placed,
        out_specs=(P("section", "row", "col"), P("section", "col", "row")),
        check_vma=False,
    )
```

```python
import jax
import jax.numpy as jnp
from jax import lax
from jax.experimental import pallas as pl
from jax.experimental.pallas import tpu as pltpu
from jax.sharding import PartitionSpec as P

NY = 4
NZ = 8
Z_PAIRS = (6, 1, 7)
Y_STEPS = (1, 3, 2)


def gelu(values):
    return jax.nn.gelu(values, approximate=True)


def gelu_grad(values, upstream):
    return jax.vjp(gelu, values)[1](upstream)[0]


def swap_col(value, dz, dy):
    pairs = []
    for z in range(NZ):
        for y in range(NY):
            pairs.append((z * NY + y, (z ^ dz) * NY + (y ^ dy)))
    return lax.ppermute(value, "col", pairs)


def swap_section(value, dz):
    cols = NZ * NY
    pairs = []
    for s in range(2):
        for z in range(NZ):
            for y in range(NY):
                pairs.append((s * cols + z * NY + y, (1 - s) * cols + (z ^ dz) * NY + y))
    return lax.ppermute(value, ("section", "col"), pairs)


def swap_row(value, by):
    return lax.ppermute(value, "row", [(r, r ^ by) for r in range(4)])


def dot(left, right, dims):
    return lax.dot_general(left, right, (dims, ((), ())), preferred_element_type=jnp.float32)


def bf16(values):
    return values.astype(jnp.bfloat16)


def f32(values):
    return values.astype(jnp.float32)


def after(value, *others):
    return lax.optimization_barrier((value, *others))


def swap_pairs(pair):
    return [pair] + [swap_col(pair, k, 0) for k in Z_PAIRS]


def gather_pairs(pair):
    return jnp.concatenate(swap_pairs(pair), 0)


def gather_all(pair):
    rows, width = pair.shape
    left, right = pair[:, : width // 2], pair[:, width // 2 :]
    left = gather_pairs(left)
    right = jnp.concatenate(swap_y([right] * NY, right), 0)
    left = swap_y([left] * NY, left)
    right = swap_pairs(right)
    quarters = []
    for k in range(NY):
        ours = [block[k * rows : (k + 1) * rows] for block in right]
        quarters.append(jnp.concatenate([left[k], jnp.concatenate(ours, 0)], 1))
    return jnp.concatenate(quarters, 0)


def swap_y(blocks, own):
    got = {0: own}
    for k in Y_STEPS:
        got[k] = swap_col(blocks[k], 0, k)
    return [got[k] for k in range(NY)]


def forward_y(one, three):
    half = one.shape[0] // 2
    return jnp.concatenate([swap_col(three[:half], 0, 1), swap_col(one[half:], 0, 3)], 0)


def sum_pairs(partial):
    rows = partial.shape[0] // 4
    total = f32(partial[:rows])
    for i, k in enumerate(Z_PAIRS):
        at = (i + 1) * rows
        total = total + f32(swap_col(partial[at : at + rows], k, 0))
    return bf16(total)


def cross(pair):
    half = pair.shape[0] // 2
    turned = jnp.concatenate([pair[half:], pair[:half]], 0)
    return f32(swap_section(pair, 0)) + f32(swap_section(turned, 2))


def reduce_row(partial, core, axis):
    shape = partial.shape
    halves = partial.reshape(*shape[:axis], 2, shape[axis] // 2, *shape[axis + 1 :])
    mine = lax.dynamic_index_in_dim(halves, core, axis, False)
    other = lax.dynamic_index_in_dim(halves, 1 - core, axis, False)
    chip = f32(mine) + f32(swap_row(other, 1))
    return chip + f32(swap_row(bf16(chip), 2))


def join_cores(mine, core, axis):
    other = swap_row(mine, 1)
    first = jnp.where(core == 0, mine, other)
    second = jnp.where(core == 0, other, mine)
    return jnp.concatenate([first, second], axis)


def choose_kernel(flag_ref, plain_ref, other_ref, out_ref):
    @pl.when(flag_ref[0] == 1)
    def _():
        out_ref[...] = plain_ref[...]

    @pl.when(flag_ref[0] == 0)
    def _():
        out_ref[...] = other_ref[...].T


def choose(flag, plain, other):
    whole = pl.BlockSpec(memory_space=pltpu.VMEM)
    return pl.pallas_call(
        choose_kernel,
        out_shape=jax.ShapeDtypeStruct(plain.shape, plain.dtype),
        in_specs=[pl.BlockSpec(memory_space=pltpu.SMEM), whole, whole],
        out_specs=whole,
        compiler_params=pltpu.CompilerParams(vmem_limit_bytes=32 * 2**20),
        cost_estimate=pl.CostEstimate(
            flops=0, bytes_accessed=6 * plain.size, transcendentals=0
        ),
        name="choose",
    )(flag, plain, other)


def body(tokens, w_up, w_down, cotangent):
    first_section = lax.axis_index("section") == 0
    core = lax.axis_index("row") % 2
    col = lax.axis_index("col")
    shard, width = tokens.shape
    up = w_up[0]
    down = w_down[0]
    hidden_width = up.shape[1]

    def pick(in_a, in_b):
        return jnp.where(first_section, in_a, in_b)

    row = lax.axis_index("row")
    z, y = col // NY, col % NY
    at = ((z % 2) * NY + y) * shard
    held = []
    for k in range(4):
        mine = lax.dynamic_slice(cotangent, (at, (row ^ k) * width), (shard, width))
        held.append(swap_row(mine, k) if k else mine)
    owner = row ^ (z // 2)
    cot_pair = []
    for i in range(2):
        got = held[0 ^ i]
        for k in (1, 2, 3):
            got = jnp.where(owner == k, held[k ^ i], got)
        cot_pair.append(got)
    cot_pair = jnp.concatenate(cot_pair, 0)
    token_pair = jnp.concatenate([tokens, swap_col(tokens, 2, 0)], 0)
    pair = pick(token_pair, cot_pair)

    flag = jnp.where(first_section, 1, 0).astype(jnp.int32)
    pair, flag = after(pair, flag)
    w_share = choose(flag.reshape(1), down, up)
    w_own = choose(flag.reshape(1), up, down)

    ahead, back = ((1,), (0,)), ((1,), (1,))

    def blocks_of(acts):
        return [acts[:, k * hidden_width : (k + 1) * hidden_width] for k in range(NY)]

    def exchange_y(acts):
        return swap_y(acts, acts[0])

    start = gather_all(pair)
    start, w_share = after(start, w_share)
    shares = {0: w_share}
    for k in (1, 3):
        shares[k] = swap_col(w_share, 0, k)
    shares[2] = forward_y(shares[1], shares[3])
    part = bf16(dot(start, w_own, ahead)).reshape(NY, -1, hidden_width)
    sum_one = reduce_row(part, core, 1)
    hidden_a = bf16(gelu(sum_one))
    moved = jnp.concatenate(exchange_y(pick(hidden_a, bf16(sum_one))), 1)
    moved, *weights = after(moved, *[shares[k] for k in range(NY)])
    weights = jnp.concatenate(weights, 0)

    def enter(acts):
        return reduce_row(bf16(dot(acts, weights, back)), core, 0)

    def leave(acts):
        return sum_pairs(bf16(dot(join_cores(acts, core, 0), weights, ahead)))

    x_b = gather_pairs(bf16(f32(token_pair) + cross(leave(moved))))
    pre_b = enter(x_b)
    hidden_b = bf16(gelu(pre_b))
    grad_pre_b = bf16(gelu_grad(pre_b, f32(moved)))
    back_part = leave(grad_pre_b)
    back_part, hidden_b = after(back_part, hidden_b)
    hidden = pick(hidden_a, jnp.stack(exchange_y(blocks_of(hidden_b)), 0))
    hidden_all = join_cores(hidden, core, 1).reshape(-1, hidden_width)

    grad_a = gather_pairs(bf16(f32(cot_pair) + cross(back_part)))
    second = pick(grad_a, x_b)
    seconds = {0: second, 1: swap_col(second, 0, 1), 3: swap_col(second, 0, 3)}
    grad_a, hidden_all = after(grad_a, hidden_all)
    last = pick(bf16(enter(grad_a)), grad_pre_b)
    last, seconds[1], seconds[3] = after(last, seconds[1], seconds[3])
    seconds[2] = forward_y(seconds[1], seconds[3])
    last = jnp.stack(exchange_y(blocks_of(last)), 0)
    grad_pre = pick(bf16(gelu_grad(sum_one, f32(last))), last)
    grad_pre_all = join_cores(grad_pre, core, 1).reshape(-1, hidden_width)

    end = jnp.concatenate([seconds[k] for k in range(NY)], 0)
    x_all, grad_all = pick(start, end), pick(end, start)
    grad_down = dot(hidden_all, grad_all, ((0,), (0,)))
    grad_up = dot(x_all, grad_pre_all, ((0,), (0,)))
    return (grad_up[None], grad_down[None])


def solution(mesh):
    placed = (
        P("col", "row"),
        P("section", "row", "col"),
        P("section", "col", "row"),
        P("row", None),
    )
    return jax.shard_map(
        body,
        mesh=mesh,
        in_specs=placed,
        out_specs=(P("section", "row", "col"), P("section", "col", "row")),
        check_vma=False,
    )
```

```python
import jax
import jax.numpy as jnp
from jax import lax
from jax.experimental import pallas as pl
from jax.experimental.pallas import tpu as pltpu
from jax.sharding import PartitionSpec as P

NY = 4
NZ = 8
Z_PAIRS = (6, 1, 7)
Y_STEPS = (1, 3, 2)


def gelu(values):
    return jax.nn.gelu(values, approximate=True)


def gelu_grad(values, upstream):
    return jax.vjp(gelu, values)[1](upstream)[0]


def swap_col(value, dz, dy):
    pairs = []
    for z in range(NZ):
        for y in range(NY):
            pairs.append((z * NY + y, (z ^ dz) * NY + (y ^ dy)))
    return lax.ppermute(value, "col", pairs)


def swap_section(value, dz):
    cols = NZ * NY
    pairs = []
    for s in range(2):
        for z in range(NZ):
            for y in range(NY):
                pairs.append((s * cols + z * NY + y, (1 - s) * cols + (z ^ dz) * NY + y))
    return lax.ppermute(value, ("section", "col"), pairs)


def swap_row(value, by):
    return lax.ppermute(value, "row", [(r, r ^ by) for r in range(4)])


def dot(left, right, dims):
    return lax.dot_general(left, right, (dims, ((), ())), preferred_element_type=jnp.float32)


def bf16(values):
    return values.astype(jnp.bfloat16)


def f32(values):
    return values.astype(jnp.float32)


def after(value, *others):
    return lax.optimization_barrier((value, *others))


def swap_pairs(pair):
    return [pair] + [swap_col(pair, k, 0) for k in Z_PAIRS]


def gather_pairs(pair):
    return jnp.concatenate(swap_pairs(pair), 0)


def swap_y(blocks, own):
    got = {0: own}
    for k in Y_STEPS:
        got[k] = swap_col(blocks[k], 0, k)
    return [got[k] for k in range(NY)]


def forward_y(one, three):
    half = one.shape[0] // 2
    return jnp.concatenate([swap_col(three[:half], 0, 1), swap_col(one[half:], 0, 3)], 0)


def sum_pairs(partial):
    rows = partial.shape[0] // 4
    total = f32(partial[:rows])
    for i, k in enumerate(Z_PAIRS):
        at = (i + 1) * rows
        total = total + f32(swap_col(partial[at : at + rows], k, 0))
    return bf16(total)


def cross(pair):
    half = pair.shape[0] // 2
    turned = jnp.concatenate([pair[half:], pair[:half]], 0)
    return f32(swap_section(pair, 0)) + f32(swap_section(turned, 2))


def reduce_row(partial, core, axis):
    shape = partial.shape
    halves = partial.reshape(*shape[:axis], 2, shape[axis] // 2, *shape[axis + 1 :])
    mine = lax.dynamic_index_in_dim(halves, core, axis, False)
    other = lax.dynamic_index_in_dim(halves, 1 - core, axis, False)
    chip = f32(mine) + f32(swap_row(other, 1))
    return chip + f32(swap_row(bf16(chip), 2))


def join_cores(mine, core, axis):
    other = swap_row(mine, 1)
    first = jnp.where(core == 0, mine, other)
    second = jnp.where(core == 0, other, mine)
    return jnp.concatenate([first, second], axis)


def choose_kernel(flag_ref, plain_ref, other_ref, out_ref):
    @pl.when(flag_ref[0] == 1)
    def _():
        out_ref[...] = plain_ref[...]

    @pl.when(flag_ref[0] == 0)
    def _():
        out_ref[...] = other_ref[...].T


def choose(flag, plain, other):
    whole = pl.BlockSpec(memory_space=pltpu.VMEM)
    return pl.pallas_call(
        choose_kernel,
        out_shape=jax.ShapeDtypeStruct(plain.shape, plain.dtype),
        in_specs=[pl.BlockSpec(memory_space=pltpu.SMEM), whole, whole],
        out_specs=whole,
        compiler_params=pltpu.CompilerParams(vmem_limit_bytes=32 * 2**20),
        cost_estimate=pl.CostEstimate(
            flops=0, bytes_accessed=6 * plain.size, transcendentals=0
        ),
        name="choose",
    )(flag, plain, other)


def body(tokens, w_up, w_down, cotangent):
    first_section = lax.axis_index("section") == 0
    core = lax.axis_index("row") % 2
    col = lax.axis_index("col")
    shard, width = tokens.shape
    up = w_up[0]
    down = w_down[0]
    hidden_width = up.shape[1]

    def pick(in_a, in_b):
        return jnp.where(first_section, in_a, in_b)

    row = lax.axis_index("row")
    z, y = col // NY, col % NY
    at = ((z % 2) * NY + y) * shard
    held = []
    for k in range(4):
        mine = lax.dynamic_slice(cotangent, (at, (row ^ k) * width), (shard, width))
        held.append(swap_row(mine, k) if k else mine)
    owner = row ^ (z // 2)
    cot_pair = []
    for i in range(2):
        got = held[0 ^ i]
        for k in (1, 2, 3):
            got = jnp.where(owner == k, held[k ^ i], got)
        cot_pair.append(got)
    cot_pair = jnp.concatenate(cot_pair, 0)
    token_pair = jnp.concatenate([tokens, swap_col(tokens, 2, 0)], 0)
    pair = pick(token_pair, cot_pair)

    flag = jnp.where(first_section, 1, 0).astype(jnp.int32)
    w_share = choose(flag.reshape(1), down, up)
    w_own = choose(flag.reshape(1), up, down)

    ahead, back = ((1,), (0,)), ((1,), (1,))

    def blocks_of(acts):
        return [acts[:, k * hidden_width : (k + 1) * hidden_width] for k in range(NY)]

    def exchange_y(acts):
        return swap_y(acts, acts[0])

    shares = {0: w_share}
    for k in (1, 3):
        shares[k] = swap_col(w_share, 0, k)
    start = gather_pairs(pair)
    start, shares[1], shares[3] = after(start, shares[1], shares[3])

    starts = {0: start, 1: swap_col(start, 0, 1), 3: swap_col(start, 0, 3)}
    near = (0, 1, 3)
    start, starts[1], starts[3] = after(start, starts[1], starts[3])
    starts[2] = swap_col(start, 0, 2)

    def project(blocks):
        return reduce_row(jnp.stack([bf16(dot(b, w_own, ahead)) for b in blocks], 0), core, 1)

    sums = dict(zip(near, project([starts[k] for k in near])))
    starts[2], one, three = after(starts[2], shares[1], shares[3])
    shares[2] = forward_y(one, three)
    sums[2] = project([starts[2]])[0]
    hiddens = {k: bf16(gelu(total)) for k, total in sums.items()}
    acts = {k: pick(hiddens[k], bf16(sums[k])) for k in sums}
    moved = {0: acts[0]}
    for k in Y_STEPS:
        moved[k] = swap_col(acts[k], 0, k)
    moved = jnp.concatenate([moved[k] for k in range(NY)], 1)
    moved, *weights = after(moved, *[shares[k] for k in range(NY)])
    weights = jnp.concatenate(weights, 0)
    hidden_a = jnp.stack([hiddens[k] for k in range(NY)], 0)
    sum_one = jnp.stack([sums[k] for k in range(NY)], 0)

    def enter(acts):
        return reduce_row(bf16(dot(acts, weights, back)), core, 0)

    def leave(acts):
        return sum_pairs(bf16(dot(join_cores(acts, core, 0), weights, ahead)))

    x_b = gather_pairs(bf16(f32(token_pair) + cross(leave(moved))))
    pre_b = enter(x_b)
    hidden_b = bf16(gelu(pre_b))
    grad_pre_b = bf16(gelu_grad(pre_b, f32(moved)))
    back_part = leave(grad_pre_b)
    back_part, hidden_b = after(back_part, hidden_b)
    hidden = pick(hidden_a, jnp.stack(exchange_y(blocks_of(hidden_b)), 0))
    hidden_all = join_cores(hidden, core, 1).reshape(-1, hidden_width)

    grad_a = gather_pairs(bf16(f32(cot_pair) + cross(back_part)))
    second = pick(grad_a, x_b)
    seconds = {0: second, 1: swap_col(second, 0, 1), 3: swap_col(second, 0, 3)}
    grad_a, hidden_all = after(grad_a, hidden_all)
    last = pick(bf16(enter(grad_a)), grad_pre_b)
    last, seconds[1], seconds[3] = after(last, seconds[1], seconds[3])
    seconds[2] = forward_y(seconds[1], seconds[3])
    last = jnp.stack(exchange_y(blocks_of(last)), 0)
    grad_pre = pick(bf16(gelu_grad(sum_one, f32(last))), last)
    grad_pre_all = join_cores(grad_pre, core, 1).reshape(-1, hidden_width)

    both = [(starts[k], seconds[k]) for k in range(NY)]
    x_all = jnp.concatenate([pick(a, b) for a, b in both], 0)
    grad_all = jnp.concatenate([pick(b, a) for a, b in both], 0)
    grad_down = dot(hidden_all, grad_all, ((0,), (0,)))
    grad_up = dot(x_all, grad_pre_all, ((0,), (0,)))
    return (grad_up[None], grad_down[None])


def solution(mesh):
    placed = (
        P("col", "row"),
        P("section", "row", "col"),
        P("section", "col", "row"),
        P("row", None),
    )
    return jax.shard_map(
        body,
        mesh=mesh,
        in_specs=placed,
        out_specs=(P("section", "row", "col"), P("section", "col", "row")),
        check_vma=False,
    )
```

```python
import jax
import jax.numpy as jnp
from jax import lax
from jax.experimental import pallas as pl
from jax.experimental.pallas import tpu as pltpu
from jax.sharding import PartitionSpec as P

NY = 4
NZ = 8
Z_PAIRS = (6, 1, 7)
Y_STEPS = (1, 3, 2)


def gelu(values):
    return jax.nn.gelu(values, approximate=True)


def gelu_grad(values, upstream):
    return jax.vjp(gelu, values)[1](upstream)[0]


def swap_col(value, dz, dy):
    pairs = []
    for z in range(NZ):
        for y in range(NY):
            pairs.append((z * NY + y, (z ^ dz) * NY + (y ^ dy)))
    return lax.ppermute(value, "col", pairs)


def swap_section(value, dz):
    cols = NZ * NY
    pairs = []
    for s in range(2):
        for z in range(NZ):
            for y in range(NY):
                pairs.append((s * cols + z * NY + y, (1 - s) * cols + (z ^ dz) * NY + y))
    return lax.ppermute(value, ("section", "col"), pairs)


def swap_row(value, by):
    return lax.ppermute(value, "row", [(r, r ^ by) for r in range(4)])


def dot(left, right, dims):
    return lax.dot_general(left, right, (dims, ((), ())), preferred_element_type=jnp.float32)


def bf16(values):
    return values.astype(jnp.bfloat16)


def f32(values):
    return values.astype(jnp.float32)


def after(value, *others):
    return lax.optimization_barrier((value, *others))


def swap_pairs(pair):
    return [pair] + [swap_col(pair, k, 0) for k in Z_PAIRS]


def gather_pairs(pair):
    return jnp.concatenate(swap_pairs(pair), 0)


def swap_y(blocks, own):
    got = {0: own}
    for k in Y_STEPS:
        got[k] = swap_col(blocks[k], 0, k)
    return [got[k] for k in range(NY)]


def forward_y(one, three):
    half = one.shape[0] // 2
    return jnp.concatenate([swap_col(three[:half], 0, 1), swap_col(one[half:], 0, 3)], 0)


def sum_pairs(partial):
    rows = partial.shape[0] // 4
    total = f32(partial[:rows])
    for i, k in enumerate(Z_PAIRS):
        at = (i + 1) * rows
        total = total + f32(swap_col(partial[at : at + rows], k, 0))
    return bf16(total)


def cross(pair):
    half = pair.shape[0] // 2
    turned = jnp.concatenate([pair[half:], pair[:half]], 0)
    return f32(swap_section(pair, 0)) + f32(swap_section(turned, 2))


def sum_cores(partial, core, axis):
    shape = partial.shape
    halves = partial.reshape(*shape[:axis], 2, shape[axis] // 2, *shape[axis + 1 :])
    mine = lax.dynamic_index_in_dim(halves, core, axis, False)
    other = lax.dynamic_index_in_dim(halves, 1 - core, axis, False)
    return f32(mine) + f32(swap_row(other, 1))


def sum_chips(chip):
    return chip + f32(swap_row(bf16(chip), 2))


def reduce_row(partial, core, axis):
    return sum_chips(sum_cores(partial, core, axis))


def join_cores(mine, core, axis):
    other = swap_row(mine, 1)
    first = jnp.where(core == 0, mine, other)
    second = jnp.where(core == 0, other, mine)
    return jnp.concatenate([first, second], axis)


def choose_kernel(flag_ref, plain_ref, other_ref, *refs):
    *outs, held_ref, sems = refs
    rows = outs[0].shape[0]

    @pl.when(flag_ref[0] == 1)
    def _():
        copies = [
            pltpu.make_async_copy(plain_ref.at[pl.ds(i * rows, rows), :], out, sems.at[i])
            for i, out in enumerate(outs)
        ]
        for copy in copies:
            copy.start()
        for copy in copies:
            copy.wait()

    @pl.when(flag_ref[0] == 0)
    def _():
        copy = pltpu.make_async_copy(other_ref, held_ref, sems.at[0])
        copy.start()
        copy.wait()
        for i, out in enumerate(outs):
            out[...] = held_ref[:, i * rows : (i + 1) * rows].T


def choose(flag, plain, other, parts):
    rows, columns = plain.shape
    return pl.pallas_call(
        choose_kernel,
        out_shape=[jax.ShapeDtypeStruct((rows // parts, columns), plain.dtype)] * parts,
        in_specs=[
            pl.BlockSpec(memory_space=pltpu.SMEM),
            pl.BlockSpec(memory_space=pl.ANY),
            pl.BlockSpec(memory_space=pl.ANY),
        ],
        out_specs=[pl.BlockSpec(memory_space=pltpu.VMEM)] * parts,
        scratch_shapes=[
            pltpu.VMEM(other.shape, other.dtype),
            pltpu.SemaphoreType.DMA((parts,)),
        ],
        compiler_params=pltpu.CompilerParams(vmem_limit_bytes=32 * 2**20),
        cost_estimate=pl.CostEstimate(
            flops=0, bytes_accessed=4 * plain.size, transcendentals=0
        ),
        name="choose",
    )(flag, plain, other)


def body(tokens, w_up, w_down, cotangent):
    first_section = lax.axis_index("section") == 0
    core = lax.axis_index("row") % 2
    col = lax.axis_index("col")
    shard, width = tokens.shape
    up = w_up[0]
    down = w_down[0]
    hidden_width = up.shape[1]

    def pick(in_a, in_b):
        return jnp.where(first_section, in_a, in_b)

    row = lax.axis_index("row")
    z, y = col // NY, col % NY
    at = ((z % 2) * NY + y) * shard
    held = []
    for k in range(4):
        mine = lax.dynamic_slice(cotangent, (at, (row ^ k) * width), (shard, width))
        held.append(swap_row(mine, k) if k else mine)
    owner = row ^ (z // 2)
    cot_pair = []
    for i in range(2):
        got = held[0 ^ i]
        for k in (1, 2, 3):
            got = jnp.where(owner == k, held[k ^ i], got)
        cot_pair.append(got)
    cot_pair = jnp.concatenate(cot_pair, 0)
    token_pair = jnp.concatenate([tokens, swap_col(tokens, 2, 0)], 0)
    pair = pick(token_pair, cot_pair)

    flag = jnp.where(first_section, 1, 0).astype(jnp.int32)
    w_share = choose(flag.reshape(1), down, up, 2)
    (w_own,) = choose(flag.reshape(1), up, down, 1)

    ahead, back = ((1,), (0,)), ((1,), (1,))

    def blocks_of(acts):
        return [acts[:, k * hidden_width : (k + 1) * hidden_width] for k in range(NY)]

    def exchange_y(acts):
        return swap_y(acts, acts[0])

    shares = {0: w_share}
    for k in (1, 3):
        shares[k] = [swap_col(part, 0, k) for part in w_share]
    start = gather_pairs(pair)
    start, *both = after(start, *shares[1], *shares[3])
    shares[1], shares[3] = both[:2], both[2:]

    starts = {0: start, 1: swap_col(start, 0, 1), 3: swap_col(start, 0, 3)}
    near = (0, 1, 3)
    start, starts[1], starts[3] = after(start, starts[1], starts[3])
    starts[2] = swap_col(start, 0, 2)

    def project(blocks):
        return sum_cores(jnp.stack([bf16(dot(b, w_own, ahead)) for b in blocks], 0), core, 1)

    chip = project([starts[k] for k in near])
    sums = dict(zip(near, sum_chips(chip)))
    far, one, three = after(starts[2], shares[1][1], shares[3][0])
    shares[2] = [swap_col(three, 0, 1), swap_col(one, 0, 3)]
    sums[2] = sum_chips(project([far]))[0]
    hiddens = {k: bf16(gelu(total)) for k, total in sums.items()}
    acts = {k: pick(hiddens[k], bf16(sums[k])) for k in sums}
    moved = {0: acts[0]}
    for k in Y_STEPS:
        moved[k] = swap_col(acts[k], 0, k)
    moved = jnp.concatenate([moved[k] for k in range(NY)], 1)
    weights = jnp.concatenate([part for k in range(NY) for part in shares[k]], 0)
    hidden_a = jnp.stack([hiddens[k] for k in range(NY)], 0)
    sum_one = jnp.stack([sums[k] for k in range(NY)], 0)

    def enter(acts):
        return reduce_row(bf16(dot(acts, weights, back)), core, 0)

    def leave(acts):
        return sum_pairs(bf16(dot(join_cores(acts, core, 0), weights, ahead)))

    x_b = gather_pairs(bf16(f32(token_pair) + cross(leave(moved))))
    pre_b = enter(x_b)
    hidden_b = bf16(gelu(pre_b))
    grad_pre_b = bf16(gelu_grad(pre_b, f32(moved)))
    back_part = leave(grad_pre_b)
    back_part, hidden_b = after(back_part, hidden_b)
    hidden = pick(hidden_a, jnp.stack(exchange_y(blocks_of(hidden_b)), 0))
    hidden_all = join_cores(hidden, core, 1).reshape(-1, hidden_width)

    grad_a = gather_pairs(bf16(f32(cot_pair) + cross(back_part)))
    second = pick(grad_a, x_b)
    seconds = {0: second, 1: swap_col(second, 0, 1), 3: swap_col(second, 0, 3)}
    grad_a, hidden_all = after(grad_a, hidden_all)
    last = pick(bf16(enter(grad_a)), grad_pre_b)
    last, seconds[1], seconds[3] = after(last, seconds[1], seconds[3])
    seconds[2] = forward_y(seconds[1], seconds[3])
    last = jnp.stack(exchange_y(blocks_of(last)), 0)
    grad_pre = pick(bf16(gelu_grad(sum_one, f32(last))), last)
    grad_pre_all = join_cores(grad_pre, core, 1).reshape(-1, hidden_width)

    both = [(starts[k], seconds[k]) for k in range(NY)]
    x_all = jnp.concatenate([pick(a, b) for a, b in both], 0)
    grad_all = jnp.concatenate([pick(b, a) for a, b in both], 0)
    grad_down = dot(hidden_all, grad_all, ((0,), (0,)))
    grad_up = dot(x_all, grad_pre_all, ((0,), (0,)))
    return (grad_up[None], grad_down[None])


def solution(mesh):
    placed = (
        P("col", "row"),
        P("section", "row", "col"),
        P("section", "col", "row"),
        P("row", None),
    )
    return jax.shard_map(
        body,
        mesh=mesh,
        in_specs=placed,
        out_specs=(P("section", "row", "col"), P("section", "col", "row")),
        check_vma=False,
    )
```

```python
import jax
import jax.numpy as jnp
from jax import lax
from jax.experimental import pallas as pl
from jax.experimental.pallas import tpu as pltpu
from jax.sharding import PartitionSpec as P

NY = 4
NZ = 8
Z_PAIRS = (6, 1, 7)
Y_STEPS = (1, 3, 2)


def gelu(values):
    return jax.nn.gelu(values, approximate=True)


def gelu_grad(values, upstream):
    return jax.vjp(gelu, values)[1](upstream)[0]


def swap_col(value, dz, dy):
    pairs = []
    for z in range(NZ):
        for y in range(NY):
            pairs.append((z * NY + y, (z ^ dz) * NY + (y ^ dy)))
    return lax.ppermute(value, "col", pairs)


def swap_section(value, dz):
    cols = NZ * NY
    pairs = []
    for s in range(2):
        for z in range(NZ):
            for y in range(NY):
                pairs.append((s * cols + z * NY + y, (1 - s) * cols + (z ^ dz) * NY + y))
    return lax.ppermute(value, ("section", "col"), pairs)


def swap_row(value, by):
    return lax.ppermute(value, "row", [(r, r ^ by) for r in range(4)])


def dot(left, right, dims):
    return lax.dot_general(left, right, (dims, ((), ())), preferred_element_type=jnp.float32)


def bf16(values):
    return values.astype(jnp.bfloat16)


def f32(values):
    return values.astype(jnp.float32)


def after(value, *others):
    return lax.optimization_barrier((value, *others))


def swap_pairs(pair):
    return [pair] + [swap_col(pair, k, 0) for k in Z_PAIRS]


def gather_pairs(pair):
    return jnp.concatenate(swap_pairs(pair), 0)


def swap_y(blocks, own):
    got = {0: own}
    for k in Y_STEPS:
        got[k] = swap_col(blocks[k], 0, k)
    return [got[k] for k in range(NY)]


def forward_y(one, three):
    half = one.shape[0] // 2
    return jnp.concatenate([swap_col(three[:half], 0, 1), swap_col(one[half:], 0, 3)], 0)


def sum_pairs(partial):
    rows = partial.shape[0] // 4
    total = f32(partial[:rows])
    for i, k in enumerate(Z_PAIRS):
        at = (i + 1) * rows
        total = total + f32(swap_col(partial[at : at + rows], k, 0))
    return bf16(total)


def cross(pair):
    half = pair.shape[0] // 2
    turned = jnp.concatenate([pair[half:], pair[:half]], 0)
    return f32(swap_section(pair, 0)) + f32(swap_section(turned, 2))


def reduce_row(partial, core, axis):
    shape = partial.shape
    halves = partial.reshape(*shape[:axis], 2, shape[axis] // 2, *shape[axis + 1 :])
    mine = lax.dynamic_index_in_dim(halves, core, axis, False)
    other = lax.dynamic_index_in_dim(halves, 1 - core, axis, False)
    chip = f32(mine) + f32(swap_row(other, 1))
    return chip + f32(swap_row(bf16(chip), 2))


def join_cores(mine, core, axis):
    other = swap_row(mine, 1)
    first = jnp.where(core == 0, mine, other)
    second = jnp.where(core == 0, other, mine)
    return jnp.concatenate([first, second], axis)


def choose_kernel(flag_ref, plain_ref, other_ref, out_ref):
    @pl.when(flag_ref[0] == 1)
    def _():
        out_ref[...] = plain_ref[...]

    @pl.when(flag_ref[0] == 0)
    def _():
        out_ref[...] = other_ref[...].T


def choose(flag, plain, other):
    whole = pl.BlockSpec(memory_space=pltpu.VMEM)
    return pl.pallas_call(
        choose_kernel,
        out_shape=jax.ShapeDtypeStruct(plain.shape, plain.dtype),
        in_specs=[pl.BlockSpec(memory_space=pltpu.SMEM), whole, whole],
        out_specs=whole,
        compiler_params=pltpu.CompilerParams(vmem_limit_bytes=32 * 2**20),
        cost_estimate=pl.CostEstimate(
            flops=0, bytes_accessed=6 * plain.size, transcendentals=0
        ),
        name="choose",
    )(flag, plain, other)


def body(tokens, w_up, w_down, cotangent):
    first_section = lax.axis_index("section") == 0
    core = lax.axis_index("row") % 2
    col = lax.axis_index("col")
    shard, width = tokens.shape
    up = w_up[0]
    down = w_down[0]
    hidden_width = up.shape[1]

    def pick(in_a, in_b):
        return jnp.where(first_section, in_a, in_b)

    row = lax.axis_index("row")
    z, y = col // NY, col % NY
    at = ((z % 2) * NY + y) * shard
    held = []
    for k in range(4):
        mine = lax.dynamic_slice(cotangent, (at, (row ^ k) * width), (shard, width))
        held.append(swap_row(mine, k) if k else mine)
    owner = row ^ (z // 2)
    cot_pair = []
    for i in range(2):
        got = held[0 ^ i]
        for k in (1, 2, 3):
            got = jnp.where(owner == k, held[k ^ i], got)
        cot_pair.append(got)
    cot_pair = jnp.concatenate(cot_pair, 0)
    token_pair = jnp.concatenate([tokens, swap_col(tokens, 2, 0)], 0)
    pair = pick(token_pair, cot_pair)

    flag = jnp.where(first_section, 1, 0).astype(jnp.int32)
    w_share = choose(flag.reshape(1), down, up)
    w_own = choose(flag.reshape(1), up, down)

    ahead, back = ((1,), (0,)), ((1,), (1,))

    def blocks_of(acts):
        return [acts[:, k * hidden_width : (k + 1) * hidden_width] for k in range(NY)]

    def exchange_y(acts):
        return swap_y(acts, acts[0])

    shares = {0: w_share}
    for k in (1, 3):
        shares[k] = swap_col(w_share, 0, k)
    start = gather_pairs(pair)
    start, shares[1], shares[3] = after(start, shares[1], shares[3])

    starts = {0: start, 1: swap_col(start, 0, 1), 3: swap_col(start, 0, 3)}
    near = (0, 1, 3)
    half = w_share.shape[0] // 2
    start, starts[1], starts[3], one, three = after(
        start, starts[1], starts[3], shares[1][half:], shares[3][:half]
    )
    starts[2] = swap_col(start, 0, 2)

    def project(blocks):
        return reduce_row(jnp.stack([bf16(dot(b, w_own, ahead)) for b in blocks], 0), core, 1)

    sums = dict(zip(near, project([starts[k] for k in near])))
    lower, upper = swap_col(three, 0, 1), swap_col(one, 0, 3)
    sums[2] = project([starts[2]])[0]
    hiddens = {k: bf16(gelu(total)) for k, total in sums.items()}
    acts = {k: pick(hiddens[k], bf16(sums[k])) for k in sums}
    acts[2], lower, upper = after(acts[2], lower, upper)
    shares[2] = jnp.concatenate([lower, upper], 0)
    moved = {0: acts[0]}
    for k in Y_STEPS:
        moved[k] = swap_col(acts[k], 0, k)
    moved = jnp.concatenate([moved[k] for k in range(NY)], 1)
    moved, *weights = after(moved, *[shares[k] for k in range(NY)])
    weights = jnp.concatenate(weights, 0)
    hidden_a = jnp.stack([hiddens[k] for k in range(NY)], 0)
    sum_one = jnp.stack([sums[k] for k in range(NY)], 0)

    def enter(acts):
        return reduce_row(bf16(dot(acts, weights, back)), core, 0)

    def leave(acts):
        return sum_pairs(bf16(dot(join_cores(acts, core, 0), weights, ahead)))

    x_b = gather_pairs(bf16(f32(token_pair) + cross(leave(moved))))
    pre_b = enter(x_b)
    hidden_b = bf16(gelu(pre_b))
    grad_pre_b = bf16(gelu_grad(pre_b, f32(moved)))
    back_part = leave(grad_pre_b)
    back_part, hidden_b = after(back_part, hidden_b)
    hidden = pick(hidden_a, jnp.stack(exchange_y(blocks_of(hidden_b)), 0))
    hidden_all = join_cores(hidden, core, 1).reshape(-1, hidden_width)

    grad_a = gather_pairs(bf16(f32(cot_pair) + cross(back_part)))
    second = pick(grad_a, x_b)
    seconds = {0: second, 1: swap_col(second, 0, 1), 3: swap_col(second, 0, 3)}
    grad_a, hidden_all = after(grad_a, hidden_all)
    last = pick(bf16(enter(grad_a)), grad_pre_b)
    last, seconds[1], seconds[3] = after(last, seconds[1], seconds[3])
    seconds[2] = forward_y(seconds[1], seconds[3])
    last = jnp.stack(exchange_y(blocks_of(last)), 0)
    grad_pre = pick(bf16(gelu_grad(sum_one, f32(last))), last)
    grad_pre_all = join_cores(grad_pre, core, 1).reshape(-1, hidden_width)

    both = [(starts[k], seconds[k]) for k in range(NY)]
    x_all = jnp.concatenate([pick(a, b) for a, b in both], 0)
    grad_all = jnp.concatenate([pick(b, a) for a, b in both], 0)
    grad_down = dot(hidden_all, grad_all, ((0,), (0,)))
    grad_up = dot(x_all, grad_pre_all, ((0,), (0,)))
    return (grad_up[None], grad_down[None])


def solution(mesh):
    placed = (
        P("col", "row"),
        P("section", "row", "col"),
        P("section", "col", "row"),
        P("row", None),
    )
    return jax.shard_map(
        body,
        mesh=mesh,
        in_specs=placed,
        out_specs=(P("section", "row", "col"), P("section", "col", "row")),
        check_vma=False,
    )
```

```python
import jax
import jax.numpy as jnp
from jax import lax
from jax.experimental import pallas as pl
from jax.experimental.pallas import tpu as pltpu
from jax.sharding import PartitionSpec as P

NY = 4
NZ = 8
Z_PAIRS = (6, 1, 7)
Y_STEPS = (1, 3, 2)


def gelu(values):
    return jax.nn.gelu(values, approximate=True)


def gelu_grad(values, upstream):
    return jax.vjp(gelu, values)[1](upstream)[0]


def swap_col(value, dz, dy):
    pairs = []
    for z in range(NZ):
        for y in range(NY):
            pairs.append((z * NY + y, (z ^ dz) * NY + (y ^ dy)))
    return lax.ppermute(value, "col", pairs)


def swap_section(value, dz):
    cols = NZ * NY
    pairs = []
    for s in range(2):
        for z in range(NZ):
            for y in range(NY):
                pairs.append((s * cols + z * NY + y, (1 - s) * cols + (z ^ dz) * NY + y))
    return lax.ppermute(value, ("section", "col"), pairs)


def swap_row(value, by):
    return lax.ppermute(value, "row", [(r, r ^ by) for r in range(4)])


def dot(left, right, dims):
    return lax.dot_general(left, right, (dims, ((), ())), preferred_element_type=jnp.float32)


def bf16(values):
    return values.astype(jnp.bfloat16)


def f32(values):
    return values.astype(jnp.float32)


def after(value, *others):
    return lax.optimization_barrier((value, *others))


def swap_pairs(pair):
    return [pair] + [swap_col(pair, k, 0) for k in Z_PAIRS]


def gather_pairs(pair):
    return jnp.concatenate(swap_pairs(pair), 0)


def swap_y(blocks, own):
    got = {0: own}
    for k in Y_STEPS:
        got[k] = swap_col(blocks[k], 0, k)
    return [got[k] for k in range(NY)]


def forward_y(one, three):
    half = one.shape[0] // 2
    return jnp.concatenate([swap_col(three[:half], 0, 1), swap_col(one[half:], 0, 3)], 0)


def sum_pairs(partial):
    rows = partial.shape[0] // 4
    total = f32(partial[:rows])
    for i, k in enumerate(Z_PAIRS):
        at = (i + 1) * rows
        total = total + f32(swap_col(partial[at : at + rows], k, 0))
    return bf16(total)


def cross(pair):
    half = pair.shape[0] // 2
    turned = jnp.concatenate([pair[half:], pair[:half]], 0)
    return f32(swap_section(pair, 0)) + f32(swap_section(turned, 2))


def reduce_row(partial, core, axis):
    shape = partial.shape
    halves = partial.reshape(*shape[:axis], 2, shape[axis] // 2, *shape[axis + 1 :])
    mine = lax.dynamic_index_in_dim(halves, core, axis, False)
    other = lax.dynamic_index_in_dim(halves, 1 - core, axis, False)
    chip = f32(mine) + f32(swap_row(other, 1))
    return chip + f32(swap_row(bf16(chip), 2))


def join_cores(mine, core, axis):
    other = swap_row(mine, 1)
    first = jnp.where(core == 0, mine, other)
    second = jnp.where(core == 0, other, mine)
    return jnp.concatenate([first, second], axis)


def choose_kernel(flag_ref, plain_ref, other_ref, out_ref):
    @pl.when(flag_ref[0] == 1)
    def _():
        out_ref[...] = plain_ref[...]

    @pl.when(flag_ref[0] == 0)
    def _():
        out_ref[...] = other_ref[...].T


def choose(flag, plain, other):
    whole = pl.BlockSpec(memory_space=pltpu.VMEM)
    return pl.pallas_call(
        choose_kernel,
        out_shape=jax.ShapeDtypeStruct(plain.shape, plain.dtype),
        in_specs=[pl.BlockSpec(memory_space=pltpu.SMEM), whole, whole],
        out_specs=whole,
        compiler_params=pltpu.CompilerParams(vmem_limit_bytes=32 * 2**20),
        cost_estimate=pl.CostEstimate(
            flops=0, bytes_accessed=6 * plain.size, transcendentals=0
        ),
        name="choose",
    )(flag, plain, other)


def body(tokens, w_up, w_down, cotangent):
    first_section = lax.axis_index("section") == 0
    core = lax.axis_index("row") % 2
    col = lax.axis_index("col")
    shard, width = tokens.shape
    up = w_up[0]
    down = w_down[0]
    hidden_width = up.shape[1]

    def pick(in_a, in_b):
        return jnp.where(first_section, in_a, in_b)

    row = lax.axis_index("row")
    z, y = col // NY, col % NY
    at = ((z % 2) * NY + y) * shard
    held = []
    for k in range(4):
        mine = lax.dynamic_slice(cotangent, (at, (row ^ k) * width), (shard, width))
        held.append(swap_row(mine, k) if k else mine)
    owner = row ^ (z // 2)
    cot_pair = []
    for i in range(2):
        got = held[0 ^ i]
        for k in (1, 2, 3):
            got = jnp.where(owner == k, held[k ^ i], got)
        cot_pair.append(got)
    cot_pair = jnp.concatenate(cot_pair, 0)
    token_pair = jnp.concatenate([tokens, swap_col(tokens, 2, 0)], 0)
    pair = pick(token_pair, cot_pair)

    flag = jnp.where(first_section, 1, 0).astype(jnp.int32)
    w_share = choose(flag.reshape(1), down, up)
    w_own = choose(flag.reshape(1), up, down)

    ahead, back = ((1,), (0,)), ((1,), (1,))

    def blocks_of(acts):
        return [acts[:, k * hidden_width : (k + 1) * hidden_width] for k in range(NY)]

    def exchange_y(acts):
        return swap_y(acts, acts[0])

    shares = {0: w_share}
    for k in (1, 3):
        shares[k] = swap_col(w_share, 0, k)
    start = gather_pairs(pair)
    start, shares[1], shares[3] = after(start, shares[1], shares[3])

    starts = {0: start, 1: swap_col(start, 0, 1), 3: swap_col(start, 0, 3)}
    near = (0, 1, 3)
    half = w_share.shape[0] // 2
    start, starts[1], starts[3], one, three = after(
        start, starts[1], starts[3], shares[1][half:], shares[3][:half]
    )
    starts[2] = swap_col(start, 0, 2)

    def project(blocks):
        return reduce_row(jnp.stack([bf16(dot(b, w_own, ahead)) for b in blocks], 0), core, 1)

    sums = dict(zip(near, project([starts[k] for k in near])))
    lower, upper = swap_col(three, 0, 1), swap_col(one, 0, 3)
    sums[2] = project([starts[2]])[0]
    hiddens = {k: bf16(gelu(total)) for k, total in sums.items()}
    acts = {k: pick(hiddens[k], bf16(sums[k])) for k in sums}
    acts[2], lower, upper = after(acts[2], lower, upper)
    shares[2] = jnp.concatenate([lower, upper], 0)
    moved = {0: acts[0]}
    for k in Y_STEPS:
        moved[k] = swap_col(acts[k], 0, k)
    moved = jnp.concatenate([moved[k] for k in range(NY)], 1)
    moved, *weights = after(moved, *[shares[k] for k in range(NY)])
    weights = jnp.concatenate(weights, 0)
    hidden_a = jnp.stack([hiddens[k] for k in range(NY)], 0)
    sum_one = jnp.stack([sums[k] for k in range(NY)], 0)

    def enter(acts):
        return reduce_row(bf16(dot(acts, weights, back)), core, 0)

    def leave(acts):
        return sum_pairs(bf16(dot(join_cores(acts, core, 0), weights, ahead)))

    x_b = gather_pairs(bf16(f32(token_pair) + cross(leave(moved))))
    pre_b = enter(x_b)
    hidden_b = bf16(gelu(pre_b))
    grad_pre_b = bf16(gelu_grad(pre_b, f32(moved)))
    back_part = leave(grad_pre_b)
    returned, hidden_b = after(cross(back_part), hidden_b)
    hidden_b = exchange_y(blocks_of(hidden_b))

    grad_a = gather_pairs(bf16(f32(cot_pair) + returned))
    grad_a, *hidden_b = after(grad_a, *hidden_b)
    hidden = pick(hidden_a, jnp.stack(hidden_b, 0))
    hidden_all = join_cores(hidden, core, 1).reshape(-1, hidden_width)
    second = pick(grad_a, x_b)
    seconds = {0: second, 1: swap_col(second, 0, 1), 3: swap_col(second, 0, 3)}
    last = pick(bf16(enter(grad_a)), grad_pre_b)
    last, hidden_all, seconds[1], seconds[3] = after(
        last, hidden_all, seconds[1], seconds[3]
    )
    seconds[2] = forward_y(seconds[1], seconds[3])
    last = jnp.stack(exchange_y(blocks_of(last)), 0)
    grad_pre = pick(bf16(gelu_grad(sum_one, f32(last))), last)
    grad_pre_all = join_cores(grad_pre, core, 1).reshape(-1, hidden_width)

    both = [(starts[k], seconds[k]) for k in range(NY)]
    x_all = jnp.concatenate([pick(a, b) for a, b in both], 0)
    grad_all = jnp.concatenate([pick(b, a) for a, b in both], 0)
    grad_down = dot(hidden_all, grad_all, ((0,), (0,)))
    grad_up = dot(x_all, grad_pre_all, ((0,), (0,)))
    return (grad_up[None], grad_down[None])


def solution(mesh):
    placed = (
        P("col", "row"),
        P("section", "row", "col"),
        P("section", "col", "row"),
        P("row", None),
    )
    return jax.shard_map(
        body,
        mesh=mesh,
        in_specs=placed,
        out_specs=(P("section", "row", "col"), P("section", "col", "row")),
        check_vma=False,
    )
```

```python
import jax
import jax.numpy as jnp
from jax import lax
from jax.experimental import pallas as pl
from jax.experimental.pallas import tpu as pltpu
from jax.sharding import PartitionSpec as P

NY = 4
NZ = 8
Z_PAIRS = ((1, 1), (-1, -1), (2, -2))
Y_STEPS = (1, 3, 2)


def gelu(values):
    return jax.nn.gelu(values, approximate=True)


def gelu_grad(values, upstream):
    return jax.vjp(gelu, values)[1](upstream)[0]


def swap_col(value, dz, dy):
    pairs = []
    for z in range(NZ):
        for y in range(NY):
            pairs.append((z * NY + y, (z ^ dz) * NY + (y ^ dy)))
    return lax.ppermute(value, "col", pairs)


def shift_z(value, steps, sign):
    pairs = []
    for z in range(NZ):
        to = (z + sign * steps[z % 2]) % NZ
        pairs += [(z * NY + y, to * NY + y) for y in range(NY)]
    return lax.ppermute(value, "col", pairs)


def swap_section(value, dz):
    cols = NZ * NY
    pairs = []
    for s in range(2):
        for z in range(NZ):
            for y in range(NY):
                pairs.append((s * cols + z * NY + y, (1 - s) * cols + (z ^ dz) * NY + y))
    return lax.ppermute(value, ("section", "col"), pairs)


def swap_row(value, by):
    return lax.ppermute(value, "row", [(r, r ^ by) for r in range(4)])


def dot(left, right, dims):
    return lax.dot_general(left, right, (dims, ((), ())), preferred_element_type=jnp.float32)


def bf16(values):
    return values.astype(jnp.bfloat16)


def f32(values):
    return values.astype(jnp.float32)


def after(value, *others):
    return lax.optimization_barrier((value, *others))


def swap_pairs(pair):
    return [pair] + [shift_z(pair, steps, 1) for steps in Z_PAIRS]


def gather_pairs(pair):
    return jnp.concatenate(swap_pairs(pair), 0)


def swap_y(blocks, own):
    got = {0: own}
    for k in Y_STEPS:
        got[k] = swap_col(blocks[k], 0, k)
    return [got[k] for k in range(NY)]


def forward_y(one, three):
    half = one.shape[0] // 2
    return jnp.concatenate([swap_col(three[:half], 0, 1), swap_col(one[half:], 0, 3)], 0)


def sum_pairs(partial):
    rows = partial.shape[0] // 4
    total = f32(partial[:rows])
    for i, steps in enumerate(Z_PAIRS):
        at = (i + 1) * rows
        total = total + f32(shift_z(partial[at : at + rows], steps, -1))
    return bf16(total)


def cross(pair):
    half = pair.shape[0] // 2
    turned = jnp.concatenate([pair[half:], pair[:half]], 0)
    return f32(swap_section(pair, 0)) + f32(swap_section(turned, 4))


def reduce_row(partial, core, axis):
    shape = partial.shape
    halves = partial.reshape(*shape[:axis], 2, shape[axis] // 2, *shape[axis + 1 :])
    mine = lax.dynamic_index_in_dim(halves, core, axis, False)
    other = lax.dynamic_index_in_dim(halves, 1 - core, axis, False)
    chip = f32(mine) + f32(swap_row(other, 1))
    return chip + f32(swap_row(bf16(chip), 2))


def join_cores(mine, core, axis):
    other = swap_row(mine, 1)
    first = jnp.where(core == 0, mine, other)
    second = jnp.where(core == 0, other, mine)
    return jnp.concatenate([first, second], axis)


def choose_kernel(flag_ref, plain_ref, other_ref, out_ref):
    @pl.when(flag_ref[0] == 1)
    def _():
        out_ref[...] = plain_ref[...]

    @pl.when(flag_ref[0] == 0)
    def _():
        out_ref[...] = other_ref[...].T


def choose(flag, plain, other):
    whole = pl.BlockSpec(memory_space=pltpu.VMEM)
    return pl.pallas_call(
        choose_kernel,
        out_shape=jax.ShapeDtypeStruct(plain.shape, plain.dtype),
        in_specs=[pl.BlockSpec(memory_space=pltpu.SMEM), whole, whole],
        out_specs=whole,
        compiler_params=pltpu.CompilerParams(vmem_limit_bytes=32 * 2**20),
        cost_estimate=pl.CostEstimate(
            flops=0, bytes_accessed=6 * plain.size, transcendentals=0
        ),
        name="choose",
    )(flag, plain, other)


def body(tokens, w_up, w_down, cotangent):
    first_section = lax.axis_index("section") == 0
    core = lax.axis_index("row") % 2
    col = lax.axis_index("col")
    shard, width = tokens.shape
    up = w_up[0]
    down = w_down[0]
    hidden_width = up.shape[1]

    def pick(in_a, in_b):
        return jnp.where(first_section, in_a, in_b)

    row = lax.axis_index("row")
    z, y = col // NY, col % NY
    at = ((z % 2) * NY + y) * shard
    held = []
    for k in range(4):
        mine = lax.dynamic_slice(cotangent, (at, (row ^ k) * width), (shard, width))
        held.append(swap_row(mine, k) if k else mine)
    owner = row ^ (z // 2)
    cot_pair = []
    for i in (0, 2):
        got = held[0 ^ i]
        for k in (1, 2, 3):
            got = jnp.where(owner == k, held[k ^ i], got)
        cot_pair.append(got)
    cot_pair = jnp.concatenate(cot_pair, 0)
    token_pair = jnp.concatenate([tokens, swap_col(tokens, 4, 0)], 0)
    pair = pick(token_pair, cot_pair)

    flag = jnp.where(first_section, 1, 0).astype(jnp.int32)
    w_share = choose(flag.reshape(1), down, up)
    w_own = choose(flag.reshape(1), up, down)

    ahead, back = ((1,), (0,)), ((1,), (1,))

    def blocks_of(acts):
        return [acts[:, k * hidden_width : (k + 1) * hidden_width] for k in range(NY)]

    def exchange_y(acts):
        return swap_y(acts, acts[0])

    shares = {0: w_share}
    for k in (1, 3):
        shares[k] = swap_col(w_share, 0, k)
    start = gather_pairs(pair)
    start, shares[1], shares[3] = after(start, shares[1], shares[3])

    starts = {0: start, 1: swap_col(start, 0, 1), 3: swap_col(start, 0, 3)}
    near = (0, 1, 3)
    half = w_share.shape[0] // 2
    start, starts[1], starts[3], one, three = after(
        start, starts[1], starts[3], shares[1][half:], shares[3][:half]
    )
    starts[2] = swap_col(start, 0, 2)

    def project(blocks):
        return reduce_row(jnp.stack([bf16(dot(b, w_own, ahead)) for b in blocks], 0), core, 1)

    sums = dict(zip(near, project([starts[k] for k in near])))
    lower, upper = swap_col(three, 0, 1), swap_col(one, 0, 3)
    sums[2] = project([starts[2]])[0]
    hiddens = {k: bf16(gelu(total)) for k, total in sums.items()}
    acts = {k: pick(hiddens[k], bf16(sums[k])) for k in sums}
    acts[2], lower, upper = after(acts[2], lower, upper)
    shares[2] = jnp.concatenate([lower, upper], 0)
    moved = {0: acts[0]}
    for k in Y_STEPS:
        moved[k] = swap_col(acts[k], 0, k)
    moved = jnp.concatenate([moved[k] for k in range(NY)], 1)
    moved, *weights = after(moved, *[shares[k] for k in range(NY)])
    weights = jnp.concatenate(weights, 0)
    hidden_a = jnp.stack([hiddens[k] for k in range(NY)], 0)
    sum_one = jnp.stack([sums[k] for k in range(NY)], 0)

    def enter(acts):
        return reduce_row(bf16(dot(acts, weights, back)), core, 0)

    def leave(acts):
        return sum_pairs(bf16(dot(join_cores(acts, core, 0), weights, ahead)))

    x_b = gather_pairs(bf16(f32(token_pair) + cross(leave(moved))))
    pre_b = enter(x_b)
    hidden_b = bf16(gelu(pre_b))
    grad_pre_b = bf16(gelu_grad(pre_b, f32(moved)))
    back_part = leave(grad_pre_b)
    returned, hidden_b = after(cross(back_part), hidden_b)
    hidden_b = exchange_y(blocks_of(hidden_b))

    grad_a = gather_pairs(bf16(f32(cot_pair) + returned))
    grad_a, *hidden_b = after(grad_a, *hidden_b)
    hidden = pick(hidden_a, jnp.stack(hidden_b, 0))
    hidden_all = join_cores(hidden, core, 1).reshape(-1, hidden_width)
    second = pick(grad_a, x_b)
    seconds = {0: second, 1: swap_col(second, 0, 1), 3: swap_col(second, 0, 3)}
    last = pick(bf16(enter(grad_a)), grad_pre_b)
    last, hidden_all, seconds[1], seconds[3] = after(
        last, hidden_all, seconds[1], seconds[3]
    )
    seconds[2] = forward_y(seconds[1], seconds[3])
    last = jnp.stack(exchange_y(blocks_of(last)), 0)
    grad_pre = pick(bf16(gelu_grad(sum_one, f32(last))), last)
    grad_pre_all = join_cores(grad_pre, core, 1).reshape(-1, hidden_width)

    both = [(starts[k], seconds[k]) for k in range(NY)]
    x_all = jnp.concatenate([pick(a, b) for a, b in both], 0)
    grad_all = jnp.concatenate([pick(b, a) for a, b in both], 0)
    grad_down = dot(hidden_all, grad_all, ((0,), (0,)))
    grad_up = dot(x_all, grad_pre_all, ((0,), (0,)))
    return (grad_up[None], grad_down[None])


def solution(mesh):
    placed = (
        P("col", "row"),
        P("section", "row", "col"),
        P("section", "col", "row"),
        P("row", None),
    )
    return jax.shard_map(
        body,
        mesh=mesh,
        in_specs=placed,
        out_specs=(P("section", "row", "col"), P("section", "col", "row")),
        check_vma=False,
    )
```
